128 devices in a mesh: enc: 8 (over y, z_hi), ctx: 16 (over x, z_lo, core).
Axes of the slice: x: 4, y: 4, z: 4 (z_hi: 2, z_lo: 2; z = z_hi * 2 + z_lo), core: 2. Of those that a mesh axis runs over, the one named last changes fastest.
Arguments:
- self_queries: bfloat16 [4096, 4096], P('ctx', 'enc'), may hold values from -88 to 88
- self_keys: bfloat16 [4096, 4096], P('ctx', 'enc'), may hold values from -5 to 5
- self_values: bfloat16 [4096, 4096], P('ctx', 'enc'), may hold values from -6 to 6
- hidden_in: bfloat16 [4096, 4096], P('ctx', 'enc'), may hold values from -6 to 6
- query_gain: bfloat16 [4096], replicated, may hold values from 0.25 to 1.75
- store_gain: bfloat16 [4096], replicated, may hold values from 0.25 to 1.75
- store_table: bfloat16 [65536, 4096], P(('enc', 'ctx')), may hold values from -6 to 6
- cross_query_weight: bfloat16 [4096, 4096], P(None, 'enc'), may hold values from -0.0625 to 0.0625
- cross_kv_weight: bfloat16 [4096, 2, 4096], P(None, None, 'enc'), may hold values from -1.9375 to 1.9375
- self_out_weight: bfloat16 [4096, 4096], P('enc'), may hold values from -0.75 to 0.75
- cross_out_weight: bfloat16 [4096, 4096], P('enc'), may hold values from -0.75 to 0.75
- neighbour_ids: int32 [64, 2, 128], P('ctx', None, 'enc'), may hold values from 0 to 65535, as said below
- neighbour_counts: int32 [64], P('ctx'), may hold values from 1 to 2
Outputs:
- layer_out: bfloat16 [4096, 4096], P('ctx', 'enc')
The draws below stay inside these ranges and needn't reach their ends.
Inputs may be any that keep to these rules, and one draw needn't show every extreme that they name: `neighbour_ids`: store shard s is the block of 512 consecutive rows held by device s in the mesh order enc, ctx. Of the ids held by one device, at most 2 fall into one shard, and in every draw some shards receive exactly 2 ids from every device.
All inputs are finite; a program needn't handle non-finite values.
Results may differ from the reference program's by a relative error of at most 0.019.
The reference program's roundings to bfloat16 on the way count: a program that leaves them out, or rounds other values in their place, can miss the bound.
Values may be sent and summed in bfloat16 or wider, within the bound.
No kernel may reach another device: no remote copies, remote signals or barrier semaphores. Data moves between devices by JAX's collectives and lax.ppermute only.
A program may use at most 192 MiB of HBM per device.

```python
import math
import jax
import jax.numpy as jnp
from jax import lax

D = 4096
HEADS = 32
HD = 128
SPAN = 64
NEIGH = 2
NLEN = 128
VOC_DEV = 512
TOK_DEV = 256
SEQ = 4096
SPANS = 64
VOCAB = 65536
N_ENC = 8
N_CTX = 16


def common_keys(key):
    return jnp.clip(jax.random.normal(jax.random.fold_in(key, 11), (SEQ, D), jnp.float32), -4.0, 4.0)


def query_matrix(key):
    fresh = jnp.clip(jax.random.normal(jax.random.fold_in(key, 23), (D, D), jnp.float32), -4.0, 4.0)
    return fresh * D ** (-0.5)


def draw_self_keys(key, part):
    shared = common_keys(key)
    return shared.astype(jnp.bfloat16)


def draw_self_queries(key, part):
    key = jax.random.fold_in(key, 2)
    fresh = jnp.clip(jax.random.normal(key, (SEQ, D), jnp.float32), -4.0, 4.0)
    return fresh.astype(jnp.bfloat16)


def draw_hidden_in(key, part):
    key = jax.random.fold_in(key, 8)
    fresh = jax.random.normal(key, (SEQ, D), jnp.float32)
    return jnp.clip(fresh, -6.0, 6.0).astype(jnp.bfloat16)


def draw_store_table(key, part):
    key = jax.random.fold_in(key, 9)
    fresh = jax.random.normal(key, (VOCAB, D), jnp.float32)
    return jnp.clip(fresh, -6.0, 6.0).astype(jnp.bfloat16)


def draw_cross_query_weight(key, part):
    matrix = query_matrix(key)
    return matrix.astype(jnp.bfloat16)


def draw_cross_kv_weight(key, part):
    key = jax.random.fold_in(key, 6)
    fresh = jnp.clip(jax.random.normal(key, (D, 2, D), jnp.float32), -4.0, 4.0) * D ** (-0.5)
    return fresh.astype(jnp.bfloat16)


def draw_neighbour_ids(key, part):
    key = jax.random.fold_in(key, 7)
    span_rows = TOK_DEV // SPAN
    token_share = NLEN // N_ENC
    wanted = span_rows * NEIGH * token_share
    device_count = N_ENC * N_CTX
    capacity = max(2, 2 * wanted // device_count)
    slot_count = device_count * capacity
    hot_count = max(1, min(4, wanted // (2 * capacity)))
    key_order, key_weight, key_score, key_shuffle, key_row = jax.random.split(key, 5)
    order = jax.random.permutation(key_order, device_count)
    hotness = jnp.any(jnp.arange(device_count)[:, None] == order[None, :hot_count], axis=1).astype(jnp.int32)
    leaning = jax.random.randint(key_weight, (device_count,), 0, 4)
    slot_owner = jnp.arange(slot_count) // capacity
    noise = jax.random.randint(key_score, (N_CTX, N_ENC, slot_count), 0, 1024)
    scores = noise + leaning[slot_owner] * 512 + hotness[slot_owner] * 8192
    scores = scores * slot_count + jnp.arange(slot_count)
    chosen = lax.top_k(scores, wanted)[1]
    shuffle = jax.random.randint(key_shuffle, (N_CTX, N_ENC, wanted), 0, 4096) * wanted + jnp.arange(wanted)
    arrangement = jnp.argsort(shuffle, axis=-1)
    chosen = jnp.take_along_axis(chosen, arrangement, axis=-1)
    owners = chosen // capacity
    local_row = jax.random.randint(key_row, owners.shape, 0, VOC_DEV)
    store_ids = owners * VOC_DEV + local_row
    store_ids = store_ids.reshape(N_CTX, N_ENC, span_rows, NEIGH, token_share).transpose(0, 2, 3, 1, 4)
    return store_ids.reshape(SPANS, NEIGH, NLEN).astype(jnp.int32)


def with_ends(entries, key, smallest, largest):
    longest = entries.shape.index(max(entries.shape))
    spots = []
    for shift in (0, 1):
        where = [jax.random.randint(jax.random.fold_in(key, axis), (), 0, length) for axis, length in enumerate(entries.shape)]
        where[longest] = (where[longest] + shift) % entries.shape[longest]
        spots.append(tuple(where))
    return entries.at[spots[0]].set(smallest).at[spots[1]].set(largest)


def block_scale(own_key, shape, cuts, smallest, top_value):
    level, own = 1.0, jax.random.fold_in(own_key, 6)
    for position, parts in cuts:
        heights = jnp.exp(jax.random.uniform(jax.random.fold_in(own, position), (parts,), jnp.float32, smallest / len(cuts), top_value / len(cuts)))
        level = level * jnp.repeat(heights, shape[position] // parts).reshape([-1 if axis == position else 1 for axis in range(len(shape))])
    return level


def centred(stream_key, extent, width, reach, cuts=(), held_as=jnp.bfloat16):
    entries = jax.random.normal(stream_key, extent, jnp.float32) * width
    if len(cuts) > 0:
        entries = block_scale(stream_key, extent, cuts, -0.22, 0.18) * entries
    return jnp.clip(entries, min=-reach, max=reach).astype(held_as)


def setup_inputs(seed: int = 0) -> dict:
    arg_keys = jax.random.split(jax.random.key(seed), 14)
    self_queries = draw_self_queries(jax.random.fold_in(arg_keys[13], 71), 0)
    self_keys = draw_self_keys(jax.random.fold_in(arg_keys[13], 71), 0)
    self_values = centred(arg_keys[2], (SEQ, D), 1.0, 6.0, ((0, 16), (1, 8)))
    hidden_in = draw_hidden_in(jax.random.fold_in(arg_keys[13], 71), 0)
    query_gain = jnp.clip(1.0 + 0.15 * jax.random.normal(arg_keys[4], (D,), jnp.float32), 0.25, 1.75).astype(jnp.bfloat16)
    store_gain = jnp.clip(1.0 + 0.15 * jax.random.normal(arg_keys[5], (D,), jnp.float32), 0.25, 1.75).astype(jnp.bfloat16)
    store_table = draw_store_table(jax.random.fold_in(arg_keys[13], 71), 0)
    cross_query_weight = draw_cross_query_weight(jax.random.fold_in(arg_keys[13], 71), 0)
    cross_kv_weight = draw_cross_kv_weight(jax.random.fold_in(arg_keys[13], 71), 0)
    self_out_weight = centred(arg_keys[9], (D, D), 64 ** -0.5, 0.75, ((0, 8),))
    cross_out_weight = centred(arg_keys[10], (D, D), 64 ** -0.5, 0.75, ((0, 8),))
    neighbour_ids = draw_neighbour_ids(jax.random.fold_in(arg_keys[13], 71), 0)
    neighbour_counts = with_ends(jax.random.randint(arg_keys[12], (SPANS,), 1, NEIGH + 1), jax.random.fold_in(arg_keys[12], 1), 1, NEIGH).astype(jnp.int32)
    return {"self_queries": self_queries, "self_keys": self_keys, "self_values": self_values, "hidden_in": hidden_in, "query_gain": query_gain, "store_gain": store_gain, "store_table": store_table, "cross_query_weight": cross_query_weight, "cross_kv_weight": cross_kv_weight, "self_out_weight": self_out_weight, "cross_out_weight": cross_out_weight, "neighbour_ids": neighbour_ids, "neighbour_counts": neighbour_counts}


EPS = 1e-06

def rms_norm(store_rows, gain):
    values = store_rows.astype(jnp.float32)
    factor = lax.rsqrt(lax.optimization_barrier(jnp.mean(values * values, axis=-1, keepdims=True)) + EPS)
    return (values * factor * gain.astype(jnp.float32)).astype(jnp.bfloat16)

def reference(self_queries, self_keys, self_values, hidden_in, query_gain, store_gain, store_table, cross_query_weight, cross_kv_weight, self_out_weight, cross_out_weight, neighbour_ids, neighbour_counts):
    score_scale = 1.0 / math.sqrt(HD)
    positions = jnp.arange(SEQ, dtype=jnp.int32)
    causal = positions[:, None] >= positions[None, :]

    def one_head(head_index):
        first_col = (head_index * HD).astype(jnp.int32)
        head_queries = lax.dynamic_slice_in_dim(self_queries, first_col, HD, 1)
        head_keys = lax.dynamic_slice_in_dim(self_keys, first_col, HD, 1)
        head_values = lax.dynamic_slice_in_dim(self_values, first_col, HD, 1)
        scores = jnp.dot(head_queries, head_keys.T, preferred_element_type=jnp.float32) * score_scale
        masked = jnp.where(causal, scores, -1e+30)
        row_top = lax.optimization_barrier(jnp.max(masked, axis=1, keepdims=True))
        weights = jnp.where(causal, jnp.exp(masked - row_top), 0.0)
        row_total = lax.optimization_barrier(jnp.sum(weights, axis=1, keepdims=True))
        context = jnp.dot(weights.astype(jnp.bfloat16), head_values, preferred_element_type=jnp.float32) / row_total
        return context.astype(jnp.bfloat16)
    per_head = lax.map(one_head, jnp.arange(HEADS, dtype=jnp.int32))
    self_context = per_head.transpose(1, 0, 2).reshape(SEQ, D)
    normed_hidden = rms_norm(hidden_in, query_gain)
    cross_queries = jnp.dot(normed_hidden, cross_query_weight, preferred_element_type=jnp.float32).astype(jnp.bfloat16)
    padded_queries = jnp.concatenate([cross_queries, jnp.zeros((SPAN - 1, D), jnp.bfloat16)], axis=0)
    kv_weight = cross_kv_weight.reshape(D, 2 * D)

    def one_span(span_index):
        store_rows = store_table[neighbour_ids[span_index].reshape(-1)]
        normed = rms_norm(store_rows, store_gain)
        key_value = jnp.dot(normed, kv_weight, preferred_element_type=jnp.float32).astype(jnp.bfloat16)
        key_value = key_value.reshape(NEIGH * NLEN, 2, HEADS, HD)
        usable = jnp.arange(NEIGH, dtype=jnp.int32)[:, None] < neighbour_counts[span_index]
        usable = jnp.broadcast_to(usable, (NEIGH, NLEN)).reshape(-1)
        first_row = (span_index * SPAN + SPAN - 1).astype(jnp.int32)
        span_queries = lax.dynamic_slice_in_dim(padded_queries, first_row, SPAN, 0)
        span_queries = span_queries.reshape(SPAN, HEADS, HD).astype(jnp.float32)
        span_keys = key_value[:, 0].astype(jnp.float32)
        span_values = key_value[:, 1].astype(jnp.float32)
        scores = jnp.einsum('qhd,khd->hqk', span_queries, span_keys) * score_scale
        masked = jnp.where(usable[None, None, :], scores, -1e+30)
        row_top = lax.optimization_barrier(jnp.max(masked, axis=2, keepdims=True))
        weights = jnp.where(usable[None, None, :], jnp.exp(masked - row_top), 0.0)
        row_total = lax.optimization_barrier(jnp.sum(weights, axis=2))
        rounded = lax.optimization_barrier(weights.astype(jnp.bfloat16))
        context = jnp.einsum('hqk,khd->qhd', rounded.astype(jnp.float32), span_values)
        context = context / row_total.T[:, :, None]
        return context.reshape(SPAN, D).astype(jnp.bfloat16)
    span_out = lax.map(one_span, jnp.arange(SPANS, dtype=jnp.int32))
    joined = jnp.concatenate([jnp.zeros((SPAN - 1, D), jnp.bfloat16), span_out.reshape(-1, D)], axis=0)
    cross_context = joined[:SEQ]
    projected = jnp.dot(self_context, self_out_weight, preferred_element_type=jnp.float32)
    projected = projected + jnp.dot(cross_context, cross_out_weight, preferred_element_type=jnp.float32)
    return (hidden_in.astype(jnp.float32) + projected).astype(jnp.bfloat16)
```

```python
import math

import jax
import jax.numpy as jnp
from jax import lax
from jax.experimental import pallas as pl
from jax.experimental.pallas import tpu as pltpu
from jax.sharding import PartitionSpec as P

HD = 128
SPAN = 64
NEIGH = 2
NLEN = 128
EPS = 1e-06

NY = 4
NX = 4
BF = jnp.bfloat16
F32 = jnp.float32


def along_y(block, step):
    route = [(y * 2 + z, (y + step) % NY * 2 + z) for y in range(NY) for z in range(2)]
    return lax.ppermute(block, "enc", route)


def swap_z_hi(block):
    return lax.ppermute(block, "enc", [(e, e ^ 1) for e in range(2 * NY)])


def along_x(block, step):
    route = [(x * 4 + r, (x + step) % NX * 4 + r) for x in range(NX) for r in range(4)]
    return lax.ppermute(block, "ctx", route)


def swap_rest(block, bits):
    return lax.ppermute(block, "ctx", [(c, c ^ bits) for c in range(4 * NX)])


def next_ctx(block, step):
    size = 4 * NX
    route = [(c, c + step) for c in range(size) if 0 <= c + step < size]
    return lax.ppermute(block, "ctx", route)


def gather_y(block):
    half = block.shape[0] // 2
    below = along_y(block, 1)
    above = along_y(block, -1)
    first = along_y(below[:half], 1)
    second = along_y(above[half:], -1)
    return block, above, jnp.concatenate([first, second], axis=0), below


def rms_norm(rows, gain):
    values = rows.astype(F32)
    factor = lax.rsqrt(jnp.mean(values * values, axis=-1, keepdims=True) + EPS)
    return (values * factor * gain.astype(F32)).astype(BF)


def fetch(wanted, store_table):
    shard_rows = store_table.shape[0]
    device_count = lax.axis_size("enc") * lax.axis_size("ctx")
    count = wanted.shape[0]
    owner = wanted // shard_rows
    local_row = wanted - owner * shard_rows
    order = jnp.arange(count, dtype=jnp.int32)
    same = (owner[:, None] == owner[None, :]) & (order[None, :] < order[:, None])
    slot = jnp.sum(same.astype(jnp.int32), axis=1)
    destination = owner * 2 + slot
    place = destination[:, None] == jnp.arange(device_count * 2, dtype=jnp.int32)[None, :]
    buffer = jnp.sum(jnp.where(place, local_row[:, None], 0), axis=0)
    asked = lax.all_to_all(
        buffer.reshape(device_count, 2), ("enc", "ctx"), split_axis=0, concat_axis=0, tiled=True
    )
    found = store_table[asked]
    answer = lax.all_to_all(found, ("enc", "ctx"), split_axis=0, concat_axis=0, tiled=True)
    return answer.reshape(device_count * 2, store_table.shape[1])[destination]


def causal_kernel(q_blocks, k_blocks, q_ref, near_ref, side_ref, far_ref, o_ref, s_ref, top_ref, acc_ref):
    rows = q_ref.shape[0]
    step = pl.program_id(0)
    mine = q_blocks[step]
    scale = 1.0 / math.sqrt(HD)
    query = q_ref[...]
    parts = [(near_ref, i) for i in range(4)] + [(side_ref, i) for i in range(4)]
    parts = parts + [(far_ref, i) for i in range(8)]
    top_ref[...] = jnp.full(top_ref.shape, -1e30, F32)
    for j, (ref, i) in enumerate(parts):
        @pl.when(k_blocks[j] <= mine)
        def _(j=j, ref=ref, i=i):
            key = ref[i * rows : (i + 1) * rows, :HD]
            s = lax.dot_general(query, key, (((1,), (1,)), ((), ())), preferred_element_type=F32) * scale
            offset = jnp.where(k_blocks[j] == mine, 0, rows)
            q_pos = lax.broadcasted_iota(jnp.int32, s.shape, 0) + offset
            k_pos = lax.broadcasted_iota(jnp.int32, s.shape, 1)
            s = jnp.where(q_pos >= k_pos, s, -1e30)
            s_ref[j] = s
            best = top_ref[...]
            for part in range(rows // HD):
                best = jnp.maximum(best, s[:, part * HD : (part + 1) * HD])
            top_ref[...] = best
    top = jnp.max(top_ref[...], axis=1, keepdims=True)
    acc_ref[...] = jnp.zeros(acc_ref.shape, F32)
    top_ref[...] = jnp.zeros(top_ref.shape, F32)
    for j, (ref, i) in enumerate(parts):
        @pl.when(k_blocks[j] <= mine)
        def _(j=j, ref=ref, i=i):
            value = ref[i * rows : (i + 1) * rows, HD:]
            w = jnp.exp(s_ref[j] - top)
            total = top_ref[...]
            for part in range(rows // HD):
                total = total + w[:, part * HD : (part + 1) * HD]
            top_ref[...] = total
            acc_ref[...] += jnp.dot(w.astype(BF), value, preferred_element_type=F32)
    total = jnp.sum(top_ref[...], axis=1, keepdims=True)
    o_ref[...] = (acc_ref[...] / total).astype(BF)


def causal_attention(queries, near, side, far, q_blocks, k_blocks, rows):
    steps = queries.shape[0] // rows
    whole = lambda a: pl.BlockSpec(a.shape, lambda i, *_: (0, 0))
    return pl.pallas_call(
        causal_kernel,
        grid_spec=pltpu.PrefetchScalarGridSpec(
            num_scalar_prefetch=2,
            grid=(steps,),
            in_specs=[
                pl.BlockSpec((rows, HD), lambda i, *_: (i, 0)),
                whole(near),
                whole(side),
                whole(far),
            ],
            out_specs=pl.BlockSpec((rows, HD), lambda i, *_: (i, 0)),
            scratch_shapes=[
                pltpu.VMEM((16, rows, rows), F32),
                pltpu.VMEM((rows, HD), F32),
                pltpu.VMEM((rows, HD), F32),
            ],
        ),
        out_shape=jax.ShapeDtypeStruct(queries.shape, BF),
        compiler_params=pltpu.CompilerParams(vmem_limit_bytes=32 * 1024 * 1024),
        cost_estimate=pl.CostEstimate(
            flops=4 * 40 * rows * rows * HD, bytes_accessed=3 * 1024 * 1024, transcendentals=40 * rows * rows
        ),
    )(q_blocks, k_blocks, queries, near, side, far)


def self_attention(self_queries, self_keys, self_values):
    rows = self_queries.shape[0]
    ctx = lax.axis_index("ctx")
    x, rest = ctx // 4, ctx % 4

    def head(k):
        col = (x + k) % NX * HD
        return jnp.concatenate(
            [lax.dynamic_slice_in_dim(a, col, HD, 1) for a in (self_queries, self_keys, self_values)], axis=1
        )

    pieces = [head(0)] + [along_x(head(k), k) for k in (1, 2, 3)]
    queries = jnp.concatenate([p[:, :HD] for p in pieces], axis=0)
    near = jnp.concatenate([p[:, HD:] for p in pieces], axis=0)
    side = swap_rest(near, 2)
    far = swap_rest(jnp.concatenate([near, side], axis=0), 1)
    source_x = jnp.stack([(x - k) % NX for k in range(4)]).astype(jnp.int32)
    q_blocks = source_x * 4 + rest
    k_blocks = jnp.concatenate([source_x * 4 + (rest ^ bits) for bits in (0, 2, 1, 3)])
    context = causal_attention(queries, near, side, far, q_blocks, k_blocks, rows)
    back = [context[:rows]] + [along_x(context[k * rows : (k + 1) * rows], -k) for k in (1, 2, 3)]
    result = jnp.zeros((rows, NX * HD), BF)
    for k in range(4):
        result = lax.dynamic_update_slice(result, back[k], (0, (x + k) % NX * HD))
    return result


def span_attention(queries, keys, values, allowed):
    spans, count = queries.shape[:2]
    blocks, _, rows = keys.shape[:3]
    keys = keys.transpose(1, 3, 0, 2, 4).reshape(spans, -1, blocks * rows, HD)
    values = values.transpose(1, 3, 0, 2, 4).reshape(spans, -1, blocks * rows, HD)
    scores = jnp.einsum("sqhd,shkd->shqk", queries, keys, preferred_element_type=F32) * (1.0 / math.sqrt(HD))
    allowed = jnp.tile(allowed, (1, blocks))[:, None, None, :]
    masked = jnp.where(allowed, scores, -1e30)
    top = jnp.max(masked, axis=3, keepdims=True)
    weights = jnp.where(allowed, jnp.exp(masked - top), 0.0)
    total = jnp.sum(weights, axis=3, keepdims=True)
    context = jnp.einsum("shqk,shkd->shqd", weights.astype(BF), values, preferred_element_type=F32) / total
    context = context.astype(BF).transpose(0, 2, 1, 3).reshape(spans * count, -1, HD)
    level = (top + jnp.log(total))[..., 0].transpose(0, 2, 1).reshape(spans * count, -1)
    return context, level


def scatter_sum(projected):
    rows, width = projected.shape
    enc = lax.axis_index("enc")
    y, z = enc // 2, enc % 2
    part = width // (2 * NY)
    half = rows // 2
    top, low = projected[:half], projected[half:]

    def take(a, yy, zz):
        return lax.dynamic_slice_in_dim(a, (yy * 2 + zz) * part, part, 1)

    def pair(a, k):
        return lax.dynamic_slice_in_dim(a, (y + k) % NY * 2 * part, 2 * part, 1)

    low_far = jnp.concatenate([take(low, yy, 1 - z) for yy in range(NY)], axis=1)
    low_near = jnp.concatenate([take(low, yy, z) for yy in range(NY)], axis=1)
    low_got = swap_z_hi(low_far.astype(BF))
    top_got = [along_y(pair(top, k).astype(BF), k) for k in (1, 3, 2)]
    low_sum = low_near + low_got.astype(F32)

    def column(k):
        return lax.dynamic_slice_in_dim(low_sum, (y + k) % NY * part, part, 1)

    last_got = [along_y(column(k).astype(BF), k) for k in (1, 3, 2)]
    top_sum = pair(top, 0)
    for got in top_got:
        top_sum = top_sum + got.astype(F32)
    far = lax.dynamic_slice_in_dim(top_sum, (1 - z) * part, part, 1)
    near = lax.dynamic_slice_in_dim(top_sum, z * part, part, 1)
    top_out = near + swap_z_hi(far.astype(BF)).astype(F32)
    low_out = column(0)
    for got in last_got:
        low_out = low_out + got.astype(F32)
    return jnp.concatenate([top_out, low_out], axis=0)


def per_device(
    self_queries,
    self_keys,
    self_values,
    hidden_in,
    query_gain,
    store_gain,
    store_table,
    cross_query_weight,
    cross_kv_weight,
    self_out_weight,
    cross_out_weight,
    neighbour_ids,
    neighbour_counts,
):
    rows, local_width = self_queries.shape
    heads = local_width // HD
    enc, ctx = lax.axis_index("enc"), lax.axis_index("ctx")
    y, z = enc // 2, enc % 2
    spans = neighbour_ids.shape[0]

    kv_weight = cross_kv_weight.reshape(cross_kv_weight.shape[0], 2 * local_width)
    part = kv_weight.shape[0] // (4 * NX)
    piece = lax.dynamic_slice_in_dim(kv_weight, (ctx ^ 2) * part, part, 0)
    route = [(e * 4 * NX + c, (e ^ 1) * 4 * NX + (c ^ 2)) for e in range(2 * NY) for c in range(4 * NX)]
    piece = lax.ppermute(piece, ("enc", "ctx"), route)
    other_weight = lax.all_gather(piece, "ctx", axis=0, tiled=True)

    own_rows = rms_norm(fetch(neighbour_ids.reshape(-1), store_table), store_gain)

    pair = swap_z_hi(hidden_in)
    pair = jnp.where(
        z == 0,
        jnp.concatenate([hidden_in, pair], axis=1),
        jnp.concatenate([pair, hidden_in], axis=1),
    )
    full_hidden = jnp.zeros((rows, NY * 2 * local_width), BF)
    for k, block in enumerate(gather_y(pair)):
        full_hidden = lax.dynamic_update_slice(full_hidden, block, (0, (y + k) % NY * 2 * local_width))
    normed_hidden = rms_norm(full_hidden, query_gain)
    cross_queries = jnp.dot(normed_hidden, cross_query_weight, preferred_element_type=F32).astype(BF)
    later = next_ctx(cross_queries[:SPAN], -1)
    own_queries = jnp.concatenate([cross_queries[SPAN - 1 :], later[: SPAN - 1]], axis=0)
    other_queries = swap_z_hi(own_queries)

    self_context = self_attention(self_queries, self_keys, self_values)

    normed = jnp.concatenate(gather_y(own_rows), axis=0)

    def attend(queries, weight):
        kv = jnp.dot(normed, weight, preferred_element_type=F32).astype(BF)
        kv = kv.reshape(NY, spans, -1, 2, heads, HD)
        allowed = jnp.arange(NEIGH, dtype=jnp.int32)[None, :, None] < neighbour_counts[:, None, None]
        allowed = jnp.broadcast_to(allowed, (spans, NEIGH, kv.shape[2] // NEIGH)).reshape(spans, -1)
        return span_attention(queries.reshape(spans, SPAN, heads, HD), kv[:, :, :, 0], kv[:, :, :, 1], allowed)

    other_context, other_level = attend(other_queries, other_weight)
    got_context = swap_z_hi(other_context.reshape(rows, local_width)).reshape(rows, heads, HD)
    got_level = swap_z_hi(other_level)
    own_context, own_level = attend(own_queries, kv_weight)
    level = jnp.maximum(own_level, got_level)
    own_share = jnp.exp(own_level - level)
    got_share = jnp.exp(got_level - level)
    whole = own_share + got_share
    context = own_context.astype(F32) * (own_share / whole)[:, :, None]
    context = context + got_context.astype(F32) * (got_share / whole)[:, :, None]
    context = context.astype(BF).reshape(rows, local_width)
    earlier = next_ctx(context[rows - SPAN :], 1)
    cross_context = jnp.concatenate([earlier[1:], context[: rows - SPAN + 1]], axis=0)

    projected = jnp.dot(self_context, self_out_weight, preferred_element_type=F32)
    projected = projected + jnp.dot(cross_context, cross_out_weight, preferred_element_type=F32)
    return (hidden_in.astype(F32) + scatter_sum(projected)).astype(BF)


def solution(mesh):
    placed = (
        P("ctx", "enc"),
        P("ctx", "enc"),
        P("ctx", "enc"),
        P("ctx", "enc"),
        P(),
        P(),
        P(("enc", "ctx"), None),
        P(None, "enc"),
        P(None, None, "enc"),
        P("enc", None),
        P("enc", None),
        P("ctx", None, "enc"),
        P("ctx"),
    )
    return jax.shard_map(
        per_device, mesh=mesh, in_specs=placed, out_specs=P("ctx", "enc"), check_vma=False
    )
```

```python
import functools
import math

import jax
import jax.numpy as jnp
from jax import lax
from jax.experimental import pallas as pl
from jax.experimental.pallas import tpu as pltpu
from jax.sharding import PartitionSpec as P

HD = 128
SPAN = 64
NEIGH = 2
NLEN = 128
EPS = 1e-06

NY = 4
NX = 4
BF = jnp.bfloat16
F32 = jnp.float32


def along_y(block, step):
    route = [(y * 2 + z, (y + step) % NY * 2 + z) for y in range(NY) for z in range(2)]
    return lax.ppermute(block, "enc", route)


def swap_z_hi(block):
    return lax.ppermute(block, "enc", [(e, e ^ 1) for e in range(2 * NY)])


def along_x(block, step):
    route = [(x * 4 + r, (x + step) % NX * 4 + r) for x in range(NX) for r in range(4)]
    return lax.ppermute(block, "ctx", route)


def swap_rest(block, bits):
    return lax.ppermute(block, "ctx", [(c, c ^ bits) for c in range(4 * NX)])


def next_ctx(block, step):
    size = 4 * NX
    route = [(c, c + step) for c in range(size) if 0 <= c + step < size]
    return lax.ppermute(block, "ctx", route)


def after(values, *done):
    return jax.tree.map(lambda value: lax.optimization_barrier((value, *done))[0], values)


def gather_along(block, along):
    return block, along(block, -1), along(block, 2), along(block, 1)


def gather_halves(top, low, along):
    below, above = (along(top, 1), along(low, 1)), (along(top, -1), along(low, -1))
    far = along(below[0], 1), along(above[1], -1)
    return (top, low) + above + far + below


def rms_norm(rows, gain):
    values = rows.astype(F32)
    factor = lax.rsqrt(jnp.mean(values * values, axis=-1, keepdims=True) + EPS)
    return (values * factor * gain.astype(F32)).astype(BF)


def ask(wanted, shard_rows):
    device_count = lax.axis_size("enc") * lax.axis_size("ctx")
    count = wanted.shape[0]
    owner = wanted // shard_rows
    local_row = wanted - owner * shard_rows
    order = jnp.arange(count, dtype=jnp.int32)
    same = (owner[:, None] == owner[None, :]) & (order[None, :] < order[:, None])
    slot = jnp.sum(same.astype(jnp.int32), axis=1)
    destination = owner * 2 + slot
    place = destination[:, None] == jnp.arange(device_count * 2, dtype=jnp.int32)[None, :]
    buffer = jnp.sum(jnp.where(place, local_row[:, None], 0), axis=0)
    asked = lax.all_to_all(
        buffer.reshape(device_count, 2), ("enc", "ctx"), split_axis=0, concat_axis=0, tiled=True
    )
    return asked.reshape(-1), destination


def lookup(asked, store_table):
    return store_table.reshape(-1, store_table.shape[1] // HD, HD)[asked]


def answer(found, destination):
    came = lax.all_to_all(found, ("enc", "ctx"), split_axis=0, concat_axis=0, tiled=True)
    half = destination.shape[0] // 2
    return [came[part].reshape(half, -1) for part in (destination[:half], destination[half:])]


def causal_kernel(q_blocks, k_blocks, q_ref, near_ref, side_ref, far_ref, o_ref, s_ref, top_ref, acc_ref):
    rows = q_ref.shape[0]
    step = pl.program_id(0)
    mine = q_blocks[step]
    scale = 1.0 / math.sqrt(HD)
    query = q_ref[...]
    parts = [(near_ref, i) for i in range(4)] + [(side_ref, i) for i in range(4)]
    parts = parts + [(far_ref, i) for i in range(8)]
    top_ref[...] = jnp.full(top_ref.shape, -1e30, F32)
    for j, (ref, i) in enumerate(parts):
        @pl.when(k_blocks[j] <= mine)
        def _(j=j, ref=ref, i=i):
            key = ref[i * rows : (i + 1) * rows, :HD]
            s = lax.dot_general(query, key, (((1,), (1,)), ((), ())), preferred_element_type=F32) * scale
            offset = jnp.where(k_blocks[j] == mine, 0, rows)
            q_pos = lax.broadcasted_iota(jnp.int32, s.shape, 0) + offset
            k_pos = lax.broadcasted_iota(jnp.int32, s.shape, 1)
            s = jnp.where(q_pos >= k_pos, s, -1e30)
            s_ref[j] = s
            best = top_ref[...]
            for part in range(rows // HD):
                best = jnp.maximum(best, s[:, part * HD : (part + 1) * HD])
            top_ref[...] = best
    top = jnp.max(top_ref[...], axis=1, keepdims=True)
    acc_ref[...] = jnp.zeros(acc_ref.shape, F32)
    top_ref[...] = jnp.zeros(top_ref.shape, F32)
    for j, (ref, i) in enumerate(parts):
        @pl.when(k_blocks[j] <= mine)
        def _(j=j, ref=ref, i=i):
            value = ref[i * rows : (i + 1) * rows, HD:]
            w = jnp.exp(s_ref[j] - top)
            total = top_ref[...]
            for part in range(rows // HD):
                total = total + w[:, part * HD : (part + 1) * HD]
            top_ref[...] = total
            acc_ref[...] += jnp.dot(w.astype(BF), value, preferred_element_type=F32)
    total = jnp.sum(top_ref[...], axis=1, keepdims=True)
    o_ref[...] = (acc_ref[...] / total).astype(BF)


def causal_attention(queries, near, side, far, q_blocks, k_blocks, rows):
    steps = queries.shape[0] // rows
    whole = lambda a: pl.BlockSpec(a.shape, lambda i, *_: (0, 0))
    return pl.pallas_call(
        causal_kernel,
        grid_spec=pltpu.PrefetchScalarGridSpec(
            num_scalar_prefetch=2,
            grid=(steps,),
            in_specs=[
                pl.BlockSpec((rows, HD), lambda i, *_: (i, 0)),
                whole(near),
                whole(side),
                whole(far),
            ],
            out_specs=pl.BlockSpec((rows, HD), lambda i, *_: (i, 0)),
            scratch_shapes=[
                pltpu.VMEM((16, rows, rows), F32),
                pltpu.VMEM((rows, HD), F32),
                pltpu.VMEM((rows, HD), F32),
            ],
        ),
        out_shape=jax.ShapeDtypeStruct(queries.shape, BF),
        compiler_params=pltpu.CompilerParams(vmem_limit_bytes=32 * 1024 * 1024),
        cost_estimate=pl.CostEstimate(
            flops=4 * 40 * rows * rows * HD, bytes_accessed=3 * 1024 * 1024, transcendentals=40 * rows * rows
        ),
    )(q_blocks, k_blocks, queries, near, side, far)


def deal_heads(self_queries, self_keys, self_values):
    x = lax.axis_index("ctx") // 4

    def head(k):
        col = (x + k) % NX * HD
        return jnp.concatenate(
            [lax.dynamic_slice_in_dim(a, col, HD, 1) for a in (self_queries, self_keys, self_values)], axis=1
        )

    return [head(0)] + [along_x(head(k), k) for k in (1, 2, 3)]


def share_keys(pieces):
    near = jnp.concatenate([p[:, HD:] for p in pieces], axis=0)
    return near, swap_rest(near, 2)


def self_attention(pieces, near, side):
    rows = pieces[0].shape[0]
    ctx = lax.axis_index("ctx")
    x, rest = ctx // 4, ctx % 4
    queries = jnp.concatenate([p[:, :HD] for p in pieces], axis=0)
    far = swap_rest(jnp.concatenate([near, side], axis=0), 1)
    source_x = jnp.stack([(x - k) % NX for k in range(4)]).astype(jnp.int32)
    q_blocks = source_x * 4 + rest
    k_blocks = jnp.concatenate([source_x * 4 + (rest ^ bits) for bits in (0, 2, 1, 3)])
    context = causal_attention(queries, near, side, far, q_blocks, k_blocks, rows)
    back = [context[:rows]] + [along_x(context[k * rows : (k + 1) * rows], -k) for k in (1, 2, 3)]
    result = jnp.zeros((rows, NX * HD), BF)
    for k in range(4):
        result = lax.dynamic_update_slice(result, back[k], (0, (x + k) % NX * HD))
    return result


def query_kernel(order, gain_ref, w_ref, *refs):
    near_refs, far_ref, out_ref, w_buf, sems = refs[:NY], refs[NY], refs[NY + 1], refs[NY + 2], refs[NY + 3]
    width = near_refs[0].shape[1]
    copies = []
    for k in range(2 * NY):
        first = pl.multiple_of(order[k] * width, width)
        copies.append(pltpu.make_async_copy(w_ref.at[pl.ds(first, width)], w_buf.at[k], sems.at[k]))
    for copy in copies:
        copy.start()

    def block(k):
        if k < NY:
            return near_refs[k][...].astype(F32)
        return far_ref[:, (k - NY) * width : (k - NY + 1) * width].astype(F32)

    square = jnp.zeros((out_ref.shape[0], 1), F32)
    for k in range(2 * NY):
        values = block(k)
        square = square + jnp.sum(values * values, axis=1, keepdims=True)
    factor = lax.rsqrt(square * (1.0 / (2 * NY * width)) + EPS)
    total = jnp.zeros(out_ref.shape, F32)
    for k in range(2 * NY):
        normed = (block(k) * factor * gain_ref[pl.ds(order[k], 1), :]).astype(BF)
        copies[k].wait()
        total = total + jnp.dot(normed, w_buf[k], preferred_element_type=F32)
    out_ref[...] = total.astype(BF)


def project_queries(near, far, gain, weight, order):
    rows, width = near[0].shape
    vmem = pl.BlockSpec(memory_space=pltpu.VMEM)
    return pl.pallas_call(
        query_kernel,
        in_specs=[pl.BlockSpec(memory_space=pltpu.SMEM), vmem, pl.BlockSpec(memory_space=pl.ANY)] + [vmem] * (NY + 1),
        out_specs=vmem,
        out_shape=jax.ShapeDtypeStruct((rows, weight.shape[1]), BF),
        scratch_shapes=[
            pltpu.VMEM((2 * NY, width, weight.shape[1]), BF),
            pltpu.SemaphoreType.DMA((2 * NY,)),
        ],
        compiler_params=pltpu.CompilerParams(vmem_limit_bytes=24 * 1024 * 1024),
        cost_estimate=pl.CostEstimate(
            flops=2 * rows * weight.size, bytes_accessed=2 * weight.size + 4 * NY * rows * width, transcendentals=rows
        ),
    )(order, gain.astype(F32).reshape(2 * NY, width), weight, *near, far)


def span_kernel(steps, order, counts, q_ref, *refs):
    n_refs, w_refs = refs[: 2 * NY], refs[2 * NY : 2 * NY + len(steps)]
    out_ref, n_buf, w_buf, acc, n_sems, w_sems = refs[2 * NY + len(steps) :]
    rows, deep = n_refs[0].shape[0], w_buf.shape[1] // 2
    n_copies = [
        pltpu.make_async_copy(ref, n_buf.at[pl.ds(i * rows, rows)], n_sems.at[i]) for i, ref in enumerate(n_refs)
    ]
    w_copies = []
    for k, (ref, first) in enumerate(zip(w_refs, steps)):
        place = w_buf.at[k // 2, pl.ds(k % 2 * deep, deep)]
        w_copies.append(pltpu.make_async_copy(ref.at[pl.ds(first, deep)], place, w_sems.at[k]))
    for copy in n_copies + w_copies:
        copy.start()
    for copy in n_copies:
        copy.wait()
    for k in range(len(steps) // 2):
        columns = [pl.ds(pl.multiple_of(order[2 * k + i] * deep, deep), deep) for i in range(2)]
        values = jnp.concatenate([n_buf[:, c] for c in columns], axis=1)
        w_copies[2 * k].wait()
        w_copies[2 * k + 1].wait()
        part = jnp.dot(values, w_buf[k], preferred_element_type=F32)
        if k == 0:
            acc[...] = part
        else:
            acc[...] += part

    queries, keys = q_ref.shape[0], acc.shape[0]
    width = q_ref.shape[1]
    heads = width // HD
    spans = queries // SPAN
    rows = keys // NY
    token_rows = rows // spans
    q_span = lax.broadcasted_iota(jnp.int32, (queries, keys), 0) // SPAN
    column = lax.broadcasted_iota(jnp.int32, (queries, keys), 1)
    k_span = column % rows // token_rows
    k_neighbour = column % token_rows // (token_rows // NEIGH)
    used = jnp.zeros((queries, keys), jnp.int32)
    for i in range(spans):
        used = jnp.where(q_span == i, counts[i], used)
    allowed = (q_span == k_span) & (k_neighbour < used)
    lane = lax.broadcasted_iota(jnp.int32, (queries, HD), 1)
    levels = jnp.zeros((queries, HD), F32)
    for h in range(heads):
        cols = slice(h * HD, (h + 1) * HD)
        key = acc[:, cols].astype(BF)
        value = acc[:, width + h * HD : width + (h + 1) * HD].astype(BF)
        s = lax.dot_general(q_ref[:, cols], key, (((1,), (1,)), ((), ())), preferred_element_type=F32)
        s = jnp.where(allowed, s * (1.0 / math.sqrt(HD)), -1e30)
        top = jnp.max(s, axis=1, keepdims=True)
        w = jnp.exp(s - top)
        total = jnp.sum(w, axis=1, keepdims=True)
        context = jnp.dot(w.astype(BF), value, preferred_element_type=F32) / total
        out_ref[:, cols] = context.astype(BF)
        level = top + jnp.log(total)
        high = level.astype(BF).astype(F32)
        levels = jnp.where(lane == h, high, levels)
        levels = jnp.where(lane == heads + h, level - high, levels)
    out_ref[:, width:] = levels.astype(BF)


def attend_spans(queries, counts, normed, weights, steps, order):
    rows, width = queries.shape
    deep = normed[0].shape[1] // len(steps)
    any_space = pl.BlockSpec(memory_space=pl.ANY)
    smem = pl.BlockSpec(memory_space=pltpu.SMEM)
    vmem = pl.BlockSpec(memory_space=pltpu.VMEM)
    key_rows = 2 * NY * normed[0].shape[0]
    depth = normed[0].shape[1]
    return pl.pallas_call(
        functools.partial(span_kernel, steps),
        in_specs=[smem, smem, vmem] + [any_space] * (2 * NY + len(steps)),
        out_specs=vmem,
        out_shape=jax.ShapeDtypeStruct((rows, width + HD), BF),
        scratch_shapes=[
            pltpu.VMEM((key_rows, depth), BF),
            pltpu.VMEM((len(steps) // 2, 2 * deep, 2 * width), BF),
            pltpu.VMEM((key_rows, 2 * width), F32),
            pltpu.SemaphoreType.DMA((2 * NY,)),
            pltpu.SemaphoreType.DMA((len(steps),)),
        ],
        compiler_params=pltpu.CompilerParams(vmem_limit_bytes=28 * 1024 * 1024),
        cost_estimate=pl.CostEstimate(
            flops=4 * key_rows * depth * width,
            bytes_accessed=2 * (key_rows * depth + 2 * depth * width),
            transcendentals=rows * key_rows * width // HD,
        ),
    )(order, counts, queries, *normed, *weights)


def merge_kernel(own_ref, got_ref, out_ref):
    width = out_ref.shape[1]
    heads = width // HD
    own_levels, got_levels = own_ref[:, width:].astype(F32), got_ref[:, width:].astype(F32)
    for h in range(heads):
        cols = slice(h * HD, (h + 1) * HD)
        own = own_levels[:, h : h + 1] + own_levels[:, heads + h : heads + h + 1]
        got = got_levels[:, h : h + 1] + got_levels[:, heads + h : heads + h + 1]
        top = jnp.maximum(own, got)
        own_share, got_share = jnp.exp(own - top), jnp.exp(got - top)
        mixed = own_ref[:, cols].astype(F32) * own_share + got_ref[:, cols].astype(F32) * got_share
        out_ref[:, cols] = (mixed / (own_share + got_share)).astype(BF)


def merge_contexts(own, got):
    vmem = pl.BlockSpec(memory_space=pltpu.VMEM)
    return pl.pallas_call(
        merge_kernel,
        in_specs=[vmem, vmem],
        out_specs=vmem,
        out_shape=jax.ShapeDtypeStruct((own.shape[0], own.shape[1] - HD), BF),
        cost_estimate=pl.CostEstimate(flops=own.size * 6, bytes_accessed=own.size * 6, transcendentals=0),
    )(own, got)


def scatter_sum(projected):
    rows, width = projected.shape
    enc = lax.axis_index("enc")
    y, z = enc // 2, enc % 2
    part = width // (2 * NY)
    half = rows // 2
    top, low = projected[:half], projected[half:]

    def take(a, yy, zz):
        return lax.dynamic_slice_in_dim(a, (yy * 2 + zz) * part, part, 1)

    def pair(a, k):
        return lax.dynamic_slice_in_dim(a, (y + k) % NY * 2 * part, 2 * part, 1)

    low_far = jnp.concatenate([take(low, yy, 1 - z) for yy in range(NY)], axis=1)
    low_near = jnp.concatenate([take(low, yy, z) for yy in range(NY)], axis=1)
    low_got = swap_z_hi(low_far.astype(BF))
    top_got = [along_y(pair(top, k).astype(BF), k) for k in (1, 3, 2)]
    low_sum = low_near + low_got.astype(F32)

    def column(k):
        return lax.dynamic_slice_in_dim(low_sum, (y + k) % NY * part, part, 1)

    last_got = [along_y(column(k).astype(BF), k) for k in (1, 3, 2)]
    top_sum = pair(top, 0)
    for got in top_got:
        top_sum = top_sum + got.astype(F32)
    far = lax.dynamic_slice_in_dim(top_sum, (1 - z) * part, part, 1)
    near = lax.dynamic_slice_in_dim(top_sum, z * part, part, 1)
    top_out = near + swap_z_hi(far.astype(BF)).astype(F32)
    low_out = column(0)
    for got in last_got:
        low_out = low_out + got.astype(F32)
    return jnp.concatenate([top_out, low_out], axis=0)


def per_device(
    self_queries,
    self_keys,
    self_values,
    hidden_in,
    query_gain,
    store_gain,
    store_table,
    cross_query_weight,
    cross_kv_weight,
    self_out_weight,
    cross_out_weight,
    neighbour_ids,
    neighbour_counts,
):
    rows, local_width = self_queries.shape
    heads = local_width // HD
    enc, ctx = lax.axis_index("enc"), lax.axis_index("ctx")
    y, z = enc // 2, enc % 2
    spans = neighbour_ids.shape[0]

    x, z_lo, core = ctx // 4, ctx // 2 % 2, ctx % 2
    depth = cross_kv_weight.shape[0] // 2
    part = depth // NX
    first = core * depth + x * part + (1 - z_lo) * (part // 2)
    piece = lax.dynamic_slice_in_dim(cross_kv_weight, first, part // 2, 0).reshape(part // 2, 2 * local_width)
    asked, destination = ask(after(neighbour_ids, piece).reshape(-1), store_table.shape[0])
    route = [(e * 4 * NX + c, (e ^ 1) * 4 * NX + (c ^ 2)) for e in range(2 * NY) for c in range(4 * NX)]
    piece = lax.ppermute(piece, ("enc", "ctx"), route)
    near_hidden = gather_along(hidden_in, along_y)

    found = lookup(after(asked, piece), store_table)
    dealt = deal_heads(*after((self_queries, self_keys, self_values), asked))
    piece = after(piece, found)
    pieces = [piece, swap_rest(piece, 2)]
    cross_kv_weight = after(cross_kv_weight, found)
    kv_weight = cross_kv_weight.reshape(2 * depth, 2 * local_width)
    own_rows = [rms_norm(half, store_gain) for half in answer(found, destination)]
    own_rows = after(own_rows, kv_weight, *pieces)
    normed = gather_halves(*own_rows, along_y)
    own_rows = own_rows[0]
    pieces = gather_halves(*after(pieces, own_rows), along_x)

    near_hidden, dealt = after((near_hidden, dealt), own_rows)
    near, side = share_keys(dealt)
    far_hidden = swap_z_hi(after(jnp.concatenate(near_hidden, axis=1), side))
    turn = jnp.stack([(y + k) % NY for k in range(NY)]).astype(jnp.int32)
    hidden_order = jnp.concatenate([turn * 2 + z, turn * 2 + 1 - z])
    cross_queries = project_queries(near_hidden, far_hidden, query_gain, cross_query_weight, hidden_order)
    later = next_ctx(cross_queries[:SPAN], -1)
    own_queries = jnp.concatenate([cross_queries[SPAN - 1 :], later[: SPAN - 1]], axis=0)
    other_queries = swap_z_hi(own_queries)

    self_context = self_attention(dealt, near, after(side, normed[2], normed[7]))
    self_projected = jnp.dot(self_context, self_out_weight, preferred_element_type=F32)
    pieces = list(pieces) + [swap_rest(block, 1) for block in pieces]
    turn = jnp.stack([(x + k) % NX for k in range(NX)]).astype(jnp.int32)
    piece_order = jnp.concatenate([turn + core * NX, turn + (1 - core) * NX])
    piece_order = jnp.stack([piece_order * 2 + z_lo, piece_order * 2 + 1 - z_lo], axis=1).reshape(-1)

    counts = neighbour_counts.astype(jnp.int32)
    other = attend_spans(other_queries, counts, normed, pieces, [0] * len(pieces), piece_order)
    got = swap_z_hi(other)
    steps = [k * part // 2 for k in range(4 * NX)]
    straight = jnp.arange(4 * NX, dtype=jnp.int32)
    own = attend_spans(own_queries, counts, normed, [kv_weight] * len(steps), steps, straight)
    context = merge_contexts(own, got)
    earlier = next_ctx(context[rows - SPAN :], 1)
    cross_context = jnp.concatenate([earlier[1:], context[: rows - SPAN + 1]], axis=0)

    projected = self_projected + jnp.dot(cross_context, cross_out_weight, preferred_element_type=F32)
    return (hidden_in.astype(F32) + scatter_sum(projected)).astype(BF)


def solution(mesh):
    placed = (
        P("ctx", "enc"),
        P("ctx", "enc"),
        P("ctx", "enc"),
        P("ctx", "enc"),
        P(),
        P(),
        P(("enc", "ctx"), None),
        P(None, "enc"),
        P(None, None, "enc"),
        P("enc", None),
        P("enc", None),
        P("ctx", None, "enc"),
        P("ctx"),
    )
    return jax.shard_map(
        per_device, mesh=mesh, in_specs=placed, out_specs=P("ctx", "enc"), check_vma=False
    )
```

```python
import functools
import math

import jax
import jax.numpy as jnp
from jax import lax
from jax.experimental import pallas as pl
from jax.experimental.pallas import tpu as pltpu
from jax.sharding import PartitionSpec as P

HD = 128
SPAN = 64
NEIGH = 2
NLEN = 128
EPS = 1e-06

NY = 4
NX = 4
BF = jnp.bfloat16
F32 = jnp.float32
SHORT = pl.CostEstimate(flops=1024, bytes_accessed=1024, transcendentals=0)


def along_y(block, step):
    route = [(y * 2 + z, (y + step) % NY * 2 + z) for y in range(NY) for z in range(2)]
    return lax.ppermute(block, "enc", route)


def swap_z_hi(block):
    return lax.ppermute(block, "enc", [(e, e ^ 1) for e in range(2 * NY)])


def along_x(block, step):
    route = [(x * 4 + r, (x + step) % NX * 4 + r) for x in range(NX) for r in range(4)]
    return lax.ppermute(block, "ctx", route)


def swap_rest(block, bits):
    return lax.ppermute(block, "ctx", [(c, c ^ bits) for c in range(4 * NX)])


def next_ctx(block, step):
    size = 4 * NX
    route = [(c, c + step) for c in range(size) if 0 <= c + step < size]
    return lax.ppermute(block, "ctx", route)


def after(values, *done):
    return jax.tree.map(lambda value: lax.optimization_barrier((value, *done))[0], values)


def gather_rows(block, done):
    half = block.shape[0] // 2
    above, below = along_y(block, -1), along_y(block, 1)
    side = swap_z_hi(block)
    onward = after((below, above), done)
    far = along_y(onward[0][:half], 1), along_y(onward[1][half:], -1)
    side_onward = after(side, done)
    side_above, side_below = along_y(side_onward, -1), along_y(side_onward, 1)
    side_far = swap_z_hi(far[0]), swap_z_hi(far[1])
    return (block, above, *far, below), (side, side_above, *side_far, side_below)


def rms_norm(rows, gain):
    values = rows.astype(F32)
    factor = lax.rsqrt(jnp.mean(values * values, axis=-1, keepdims=True) + EPS)
    return (values * factor * gain.astype(F32)).astype(BF)


def ask(wanted, shard_rows):
    device_count = lax.axis_size("enc") * lax.axis_size("ctx")
    count = wanted.shape[0]
    owner = wanted // shard_rows
    local_row = wanted - owner * shard_rows
    order = jnp.arange(count, dtype=jnp.int32)
    same = (owner[:, None] == owner[None, :]) & (order[None, :] < order[:, None])
    slot = jnp.sum(same.astype(jnp.int32), axis=1)
    destination = owner * 2 + slot
    place = destination[:, None] == jnp.arange(device_count * 2, dtype=jnp.int32)[None, :]
    buffer = jnp.sum(jnp.where(place, local_row[:, None], 0), axis=0)
    return buffer.reshape(device_count, 2), destination


def lookup(asked, store_table):
    return store_table.reshape(-1, store_table.shape[1] // HD, HD)[asked]


def answer(found, destination):
    came = lax.all_to_all(found, ("enc", "ctx"), split_axis=0, concat_axis=0, tiled=True)
    return came[destination].reshape(destination.shape[0], -1)


def causal_kernel(q_blocks, k_blocks, q_ref, near_ref, side_ref, far_ref, o_ref, s_ref, top_ref, acc_ref):
    rows = q_ref.shape[0]
    step = pl.program_id(0)
    mine = q_blocks[step]
    scale = 1.0 / math.sqrt(HD)
    query = q_ref[...]
    parts = [(near_ref, i) for i in range(4)] + [(side_ref, i) for i in range(4)]
    parts = parts + [(far_ref, i) for i in range(8)]
    top_ref[...] = jnp.full(top_ref.shape, -1e30, F32)
    for j, (ref, i) in enumerate(parts):
        @pl.when(k_blocks[j] <= mine)
        def _(j=j, ref=ref, i=i):
            key = ref[i * rows : (i + 1) * rows, :HD]
            s = lax.dot_general(query, key, (((1,), (1,)), ((), ())), preferred_element_type=F32) * scale
            offset = jnp.where(k_blocks[j] == mine, 0, rows)
            q_pos = lax.broadcasted_iota(jnp.int32, s.shape, 0) + offset
            k_pos = lax.broadcasted_iota(jnp.int32, s.shape, 1)
            s = jnp.where(q_pos >= k_pos, s, -1e30)
            s_ref[j] = s
            best = top_ref[...]
            for part in range(rows // HD):
                best = jnp.maximum(best, s[:, part * HD : (part + 1) * HD])
            top_ref[...] = best
    top = jnp.max(top_ref[...], axis=1, keepdims=True)
    acc_ref[...] = jnp.zeros(acc_ref.shape, F32)
    top_ref[...] = jnp.zeros(top_ref.shape, F32)
    for j, (ref, i) in enumerate(parts):
        @pl.when(k_blocks[j] <= mine)
        def _(j=j, ref=ref, i=i):
            value = ref[i * rows : (i + 1) * rows, HD:]
            w = jnp.exp(s_ref[j] - top)
            total = top_ref[...]
            for part in range(rows // HD):
                total = total + w[:, part * HD : (part + 1) * HD]
            top_ref[...] = total
            acc_ref[...] += jnp.dot(w.astype(BF), value, preferred_element_type=F32)
    total = jnp.sum(top_ref[...], axis=1, keepdims=True)
    o_ref[...] = (acc_ref[...] / total).astype(BF)


def causal_attention(queries, near, side, far, q_blocks, k_blocks, rows):
    steps = queries.shape[0] // rows
    whole = lambda a: pl.BlockSpec(a.shape, lambda i, *_: (0, 0))
    return pl.pallas_call(
        causal_kernel,
        grid_spec=pltpu.PrefetchScalarGridSpec(
            num_scalar_prefetch=2,
            grid=(steps,),
            in_specs=[
                pl.BlockSpec((rows, HD), lambda i, *_: (i, 0)),
                whole(near),
                whole(side),
                whole(far),
            ],
            out_specs=pl.BlockSpec((rows, HD), lambda i, *_: (i, 0)),
            scratch_shapes=[
                pltpu.VMEM((16, rows, rows), F32),
                pltpu.VMEM((rows, HD), F32),
                pltpu.VMEM((rows, HD), F32),
            ],
        ),
        out_shape=jax.ShapeDtypeStruct(queries.shape, BF),
        compiler_params=pltpu.CompilerParams(vmem_limit_bytes=32 * 1024 * 1024),
        cost_estimate=SHORT,
    )(q_blocks, k_blocks, queries, near, side, far)


def deal_heads(self_queries, self_keys, self_values):
    x = lax.axis_index("ctx") // 4

    def head(k):
        col = (x + k) % NX * HD
        return jnp.concatenate(
            [lax.dynamic_slice_in_dim(a, col, HD, 1) for a in (self_queries, self_keys, self_values)], axis=1
        )

    return [head(0)] + [along_x(head(k), k) for k in (1, 2, 3)]


def near_attention(pieces, near, side):
    rows = pieces[0].shape[0]
    ctx = lax.axis_index("ctx")
    x, rest = ctx // 4, ctx % 4
    queries = jnp.concatenate([p[:, :HD] for p in pieces], axis=0)
    far = swap_rest(jnp.concatenate([near, side], axis=0), 1)
    source_x = jnp.stack([(x - k) % NX for k in range(4)]).astype(jnp.int32)
    q_blocks = source_x * 4 + rest
    k_blocks = jnp.concatenate([source_x * 4 + (rest ^ bits) for bits in (0, 2, 1, 3)])
    return causal_attention(queries, near, side, far, q_blocks, k_blocks, rows)


def return_heads(context):
    x = lax.axis_index("ctx") // 4
    rows = context.shape[0] // NX
    back = [context[:rows]] + [along_x(context[k * rows : (k + 1) * rows], -k) for k in (1, 2, 3)]
    result = jnp.zeros((rows, NX * HD), BF)
    for k in range(4):
        result = lax.dynamic_update_slice(result, back[k], (0, (x + k) % NX * HD))
    return result


def query_kernel(order, gain_ref, w_ref, *refs):
    count = 2 * NY
    piece_refs, (out_ref, w_buf, sems) = refs[:-3], refs[-3:]
    width = w_buf.shape[1]
    copies = []
    for k in range(count):
        first = pl.multiple_of(order[k] * width, width)
        copies.append(pltpu.make_async_copy(w_ref.at[pl.ds(first, width)], w_buf.at[k], sems.at[k]))
    for copy in copies:
        copy.start()

    def block(k):
        return piece_refs[k // NY][:, k % NY * width : (k % NY + 1) * width].astype(F32)

    square = jnp.zeros((out_ref.shape[0], 1), F32)
    for k in range(count):
        values = block(k)
        square = square + jnp.sum(values * values, axis=1, keepdims=True)
    factor = lax.rsqrt(square * (1.0 / (count * width)) + EPS)
    total = jnp.zeros(out_ref.shape, F32)
    for k in range(count):
        normed = (block(k) * factor * gain_ref[pl.ds(order[k], 1), :]).astype(BF)
        copies[k].wait()
        total = total + jnp.dot(normed, w_buf[k], preferred_element_type=F32)
    out_ref[...] = total.astype(BF)


def project_queries(pieces, gain, weight, order):
    rows, width = pieces[0].shape[0], pieces[0].shape[1] // NY
    vmem = pl.BlockSpec(memory_space=pltpu.VMEM)
    return pl.pallas_call(
        query_kernel,
        in_specs=[pl.BlockSpec(memory_space=pltpu.SMEM), vmem, pl.BlockSpec(memory_space=pl.ANY)] + [vmem] * len(pieces),
        out_specs=vmem,
        out_shape=jax.ShapeDtypeStruct((rows, weight.shape[1]), BF),
        scratch_shapes=[
            pltpu.VMEM((2 * NY, width, weight.shape[1]), BF),
            pltpu.SemaphoreType.DMA((2 * NY,)),
        ],
        compiler_params=pltpu.CompilerParams(vmem_limit_bytes=24 * 1024 * 1024),
        cost_estimate=SHORT,
    )(order, gain.astype(F32).reshape(2 * NY, width), weight, *pieces)


def project_rows(n_refs, w_ref, n_buf, w_buf, acc, n_sems, w_sems):
    deep = w_buf.shape[1]
    copies, first = [], 0
    for i, ref in enumerate(n_refs):
        copies.append(pltpu.make_async_copy(ref, n_buf.at[pl.ds(first, ref.shape[0])], n_sems.at[i]))
        first += ref.shape[0]
    w_copies = [
        pltpu.make_async_copy(w_ref.at[pl.ds(k * deep, deep)], w_buf.at[k], w_sems.at[k]) for k in range(w_buf.shape[0])
    ]
    for copy in copies + w_copies:
        copy.start()
    for copy in copies:
        copy.wait()
    for k, copy in enumerate(w_copies):
        copy.wait()
        part = jnp.dot(n_buf[:, k * deep : (k + 1) * deep], w_buf[k], preferred_element_type=F32)
        if k == 0:
            acc[...] = part
        else:
            acc[...] += part


def rows_kernel(w_ref, *refs):
    n_refs, (out_ref, *scratch) = refs[:-6], refs[-6:]
    project_rows(n_refs, w_ref, *scratch)
    out_ref[...] = scratch[2][...].astype(BF)


def span_kernel(counts, q_ref, kv_ref, w_ref, *refs):
    n_refs, (out_ref, tail_ref, *scratch) = refs[:-7], refs[-7:]
    project_rows(n_refs, w_ref, *scratch)
    acc = scratch[2]
    queries, keys = q_ref.shape[0], acc.shape[0]
    width = q_ref.shape[1]
    heads = width // HD
    spans = queries // SPAN
    rows = keys // NY
    token_rows = rows // spans
    q_span = lax.broadcasted_iota(jnp.int32, (queries, keys), 0) // SPAN
    column = lax.broadcasted_iota(jnp.int32, (queries, keys), 1)
    k_span = column % rows // token_rows
    k_neighbour = column % token_rows // (token_rows // NEIGH)
    used = jnp.zeros((queries, keys), jnp.int32)
    for i in range(spans):
        used = jnp.where(q_span == i, counts[i], used)
    allowed = (q_span == k_span) & (k_neighbour < used)

    def score(query, key):
        s = lax.dot_general(query, key, (((1,), (1,)), ((), ())), preferred_element_type=F32)
        return jnp.where(allowed, s * (1.0 / math.sqrt(HD)), -1e30)

    for h in range(heads):
        cols = slice(h * HD, (h + 1) * HD)
        value_cols = slice(width + h * HD, width + (h + 1) * HD)
        query = q_ref[:, cols]
        first, second = score(query, kv_ref[:, cols]), score(query, acc[:, cols].astype(BF))
        top = jnp.max(jnp.maximum(first, second), axis=1, keepdims=True)
        first, second = jnp.exp(first - top), jnp.exp(second - top)
        total = jnp.sum(first + second, axis=1, keepdims=True)
        context = jnp.dot(first.astype(BF), kv_ref[:, value_cols], preferred_element_type=F32)
        context = context + jnp.dot(
            second.astype(BF), acc[:, value_cols].astype(BF), preferred_element_type=F32
        )
        context = (context / total).astype(BF)
        out_ref[:, cols] = context
        tail_ref[:, cols] = context[queries - SPAN :]


def rows_scratch(normed, weight, steps=8):
    key_rows = sum(piece.shape[0] for piece in normed)
    depth, width = weight.shape
    return [
        pltpu.VMEM((key_rows, depth), BF),
        pltpu.VMEM((steps, depth // steps, width), BF),
        pltpu.VMEM((key_rows, width), F32),
        pltpu.SemaphoreType.DMA((len(normed),)),
        pltpu.SemaphoreType.DMA((steps,)),
    ]


def keys_values(weight, normed):
    any_space = pl.BlockSpec(memory_space=pl.ANY)
    key_rows = sum(piece.shape[0] for piece in normed)
    return pl.pallas_call(
        rows_kernel,
        in_specs=[any_space] * (1 + len(normed)),
        out_specs=pl.BlockSpec(memory_space=pltpu.VMEM),
        out_shape=jax.ShapeDtypeStruct((key_rows, weight.shape[1]), BF),
        scratch_shapes=rows_scratch(normed, weight),
        compiler_params=pltpu.CompilerParams(vmem_limit_bytes=28 * 1024 * 1024),
        cost_estimate=SHORT,
    )(weight, *normed)


def attend_spans(queries, counts, kv, weight, normed):
    rows, width = queries.shape
    any_space = pl.BlockSpec(memory_space=pl.ANY)
    vmem = pl.BlockSpec(memory_space=pltpu.VMEM)
    return pl.pallas_call(
        span_kernel,
        in_specs=[pl.BlockSpec(memory_space=pltpu.SMEM), vmem, vmem] + [any_space] * (1 + len(normed)),
        out_specs=(vmem, vmem),
        out_shape=(jax.ShapeDtypeStruct((rows, width), BF), jax.ShapeDtypeStruct((SPAN, width), BF)),
        scratch_shapes=rows_scratch(normed, weight),
        compiler_params=pltpu.CompilerParams(vmem_limit_bytes=32 * 1024 * 1024),
        cost_estimate=SHORT,
    )(counts, queries, kv, weight, *normed)


def scatter_sum(projected):
    rows, width = projected.shape
    enc = lax.axis_index("enc")
    y, z = enc // 2, enc % 2
    part = width // (2 * NY)
    half = rows // 2
    top, low = projected[:half], projected[half:]

    def take(a, yy, zz):
        return lax.dynamic_slice_in_dim(a, (yy * 2 + zz) * part, part, 1)

    def pair(a, k):
        return lax.dynamic_slice_in_dim(a, (y + k) % NY * 2 * part, 2 * part, 1)

    low_far = jnp.concatenate([take(low, yy, 1 - z) for yy in range(NY)], axis=1)
    low_near = jnp.concatenate([take(low, yy, z) for yy in range(NY)], axis=1)
    low_got = swap_z_hi(low_far.astype(BF))
    top_got = [along_y(pair(top, k).astype(BF), k) for k in (1, 3, 2)]
    low_sum = low_near + low_got.astype(F32)

    def column(k):
        return lax.dynamic_slice_in_dim(low_sum, (y + k) % NY * part, part, 1)

    last_got = [along_y(column(k).astype(BF), k) for k in (1, 3, 2)]
    top_sum = pair(top, 0)
    for got in top_got:
        top_sum = top_sum + got.astype(F32)
    far = lax.dynamic_slice_in_dim(top_sum, (1 - z) * part, part, 1)
    near = lax.dynamic_slice_in_dim(top_sum, z * part, part, 1)
    top_out = near + swap_z_hi(far.astype(BF)).astype(F32)
    low_out = column(0)
    for got in last_got:
        low_out = low_out + got.astype(F32)
    return jnp.concatenate([top_out, low_out], axis=0)


def per_device(
    self_queries,
    self_keys,
    self_values,
    hidden_in,
    query_gain,
    store_gain,
    store_table,
    cross_query_weight,
    cross_kv_weight,
    self_out_weight,
    cross_out_weight,
    neighbour_ids,
    neighbour_counts,
):
    rows, local_width = self_queries.shape
    enc = lax.axis_index("enc")
    y, z = enc // 2, enc % 2

    request, destination = ask(neighbour_ids.reshape(-1), store_table.shape[0])
    asked = lax.all_to_all(request, ("enc", "ctx"), split_axis=0, concat_axis=0, tiled=True).reshape(-1)
    dealt = deal_heads(*after((self_queries, self_keys, self_values), request))
    near = jnp.concatenate([p[:, HD:] for p in dealt], axis=0)
    found = lookup(after(asked, near), store_table)
    near, hidden, cross_kv_weight = after((near, hidden_in, cross_kv_weight), found)
    side = swap_rest(near, 2)
    hidden = [hidden, along_y(hidden, -1), along_y(hidden, 2), along_y(hidden, 1)]
    kv_weight = cross_kv_weight.reshape(-1, 2 * local_width)

    own_rows = rms_norm(answer(found, destination), store_gain)
    own_rows = after(own_rows, kv_weight, side, *hidden)
    near, side, hidden = after((near, side, hidden), own_rows)
    near_context = near_attention(dealt, near, side)
    normed, side_normed = gather_rows(own_rows, near_context)
    kv = keys_values(kv_weight, normed)
    self_context = return_heads(after(near_context, kv))
    self_projected = jnp.dot(self_context, self_out_weight, preferred_element_type=F32)

    hidden = jnp.concatenate(after(hidden, near_context), axis=1)
    far_hidden = swap_z_hi(after(hidden, side_normed[0]))
    turn = jnp.stack([(y + k) % NY for k in range(NY)]).astype(jnp.int32)
    hidden_order = jnp.concatenate([turn * 2 + z, turn * 2 + 1 - z])
    cross_queries = project_queries([hidden, far_hidden], query_gain, cross_query_weight, hidden_order)
    later = next_ctx(cross_queries[:SPAN], -1)
    queries = jnp.concatenate([cross_queries[SPAN - 1 :], later[: SPAN - 1]], axis=0)

    counts = neighbour_counts.astype(jnp.int32)
    queries = after(queries, kv, self_projected)
    context, tail = attend_spans(queries, counts, kv, kv_weight, side_normed)
    earlier = next_ctx(tail, 1)
    cross_context = jnp.concatenate([earlier[1:], context[: rows - SPAN + 1]], axis=0)

    projected = self_projected + jnp.dot(cross_context, cross_out_weight, preferred_element_type=F32)
    return (hidden_in.astype(F32) + scatter_sum(projected)).astype(BF)


def solution(mesh):
    placed = (
        P("ctx", "enc"),
        P("ctx", "enc"),
        P("ctx", "enc"),
        P("ctx", "enc"),
        P(),
        P(),
        P(("enc", "ctx"), None),
        P(None, "enc"),
        P(None, None, "enc"),
        P("enc", None),
        P("enc", None),
        P("ctx", None, "enc"),
        P("ctx"),
    )
    return jax.shard_map(
        per_device, mesh=mesh, in_specs=placed, out_specs=P("ctx", "enc"), check_vma=False
    )
```

```python
import functools
import math

import jax
import jax.numpy as jnp
from jax import lax
from jax.experimental import pallas as pl
from jax.experimental.pallas import tpu as pltpu
from jax.sharding import PartitionSpec as P

HD = 128
SPAN = 64
NEIGH = 2
NLEN = 128
EPS = 1e-06

NY = 4
NX = 4
BF = jnp.bfloat16
F32 = jnp.float32
SHORT = pl.CostEstimate(flops=1024, bytes_accessed=1024, transcendentals=0)
LONG = pl.CostEstimate(flops=1 << 36, bytes_accessed=1 << 28, transcendentals=0)


def along_y(block, step):
    route = [(y * 2 + z, (y + step) % NY * 2 + z) for y in range(NY) for z in range(2)]
    return lax.ppermute(block, "enc", route)


def swap_z_hi(block):
    return lax.ppermute(block, "enc", [(e, e ^ 1) for e in range(2 * NY)])


def along_x(block, step):
    route = [(x * 4 + r, (x + step) % NX * 4 + r) for x in range(NX) for r in range(4)]
    return lax.ppermute(block, "ctx", route)


def swap_rest(block, bits):
    return lax.ppermute(block, "ctx", [(c, c ^ bits) for c in range(4 * NX)])


def next_ctx(block, step):
    size = 4 * NX
    route = [(c, c + step) for c in range(size) if 0 <= c + step < size]
    return lax.ppermute(block, "ctx", route)


def after(values, *done):
    return jax.tree.map(lambda value: lax.optimization_barrier((value, *done))[0], values)


def gather_rows(block, fellow, done):
    half = block.shape[0] // 2
    above, below = along_y(block, -1), along_y(block, 1)
    swapped = swap_z_hi(jnp.concatenate([block, fellow], axis=0))
    side = swapped[: 2 * half]
    onward = after((below, above), done)
    far = along_y(onward[0][:half], 1), along_y(onward[1][half:], -1)
    far = jnp.concatenate(far, axis=0)
    side_above, side_below = along_y(side, -1), along_y(side, 1)
    return (block, above, far, below), (side, side_above, swap_z_hi(far), side_below), swapped[2 * half :]


def rms_norm(rows, gain):
    values = rows.astype(F32)
    factor = lax.rsqrt(jnp.mean(values * values, axis=-1, keepdims=True) + EPS)
    return (values * factor * gain.astype(F32)).astype(BF)


def ask(wanted, shard_rows):
    device_count = lax.axis_size("enc") * lax.axis_size("ctx")
    count = wanted.shape[0]
    owner = wanted // shard_rows
    local_row = wanted - owner * shard_rows
    order = jnp.arange(count, dtype=jnp.int32)
    same = (owner[:, None] == owner[None, :]) & (order[None, :] < order[:, None])
    slot = jnp.sum(same.astype(jnp.int32), axis=1)
    destination = owner * 2 + slot
    place = destination[:, None] == jnp.arange(device_count * 2, dtype=jnp.int32)[None, :]
    buffer = jnp.sum(jnp.where(place, local_row[:, None], 0), axis=0)
    return buffer.reshape(device_count, 2), destination


def lookup(asked, store_table):
    return store_table.reshape(-1, store_table.shape[1] // HD, HD)[asked]


def answer(found, destination):
    came = lax.all_to_all(found, ("enc", "ctx"), split_axis=0, concat_axis=0, tiled=True)
    return came[destination].reshape(destination.shape[0], -1)


def causal_kernel(q_blocks, k_blocks, q_ref, near_ref, side_ref, far_ref, o_ref, s_ref, top_ref, acc_ref):
    rows = q_ref.shape[0]
    step = pl.program_id(0)
    mine = q_blocks[step]
    scale = 1.0 / math.sqrt(HD)
    query = q_ref[...]
    parts = [(near_ref, i) for i in range(4)] + [(side_ref, i) for i in range(4)]
    parts = parts + [(far_ref, i) for i in range(8)]
    top_ref[...] = jnp.full(top_ref.shape, -1e30, F32)
    for j, (ref, i) in enumerate(parts):
        @pl.when(k_blocks[j] <= mine)
        def _(j=j, ref=ref, i=i):
            key = ref[i * rows : (i + 1) * rows, :HD]
            s = lax.dot_general(query, key, (((1,), (1,)), ((), ())), preferred_element_type=F32) * scale
            offset = jnp.where(k_blocks[j] == mine, 0, rows)
            q_pos = lax.broadcasted_iota(jnp.int32, s.shape, 0) + offset
            k_pos = lax.broadcasted_iota(jnp.int32, s.shape, 1)
            s = jnp.where(q_pos >= k_pos, s, -1e30)
            s_ref[j] = s
            best = top_ref[...]
            for part in range(rows // HD):
                best = jnp.maximum(best, s[:, part * HD : (part + 1) * HD])
            top_ref[...] = best
    top = jnp.max(top_ref[...], axis=1, keepdims=True)
    acc_ref[...] = jnp.zeros(acc_ref.shape, F32)
    top_ref[...] = jnp.zeros(top_ref.shape, F32)
    for j, (ref, i) in enumerate(parts):
        @pl.when(k_blocks[j] <= mine)
        def _(j=j, ref=ref, i=i):
            value = ref[i * rows : (i + 1) * rows, HD:]
            w = jnp.exp(s_ref[j] - top)
            total = top_ref[...]
            for part in range(rows // HD):
                total = total + w[:, part * HD : (part + 1) * HD]
            top_ref[...] = total
            acc_ref[...] += jnp.dot(w.astype(BF), value, preferred_element_type=F32)
    total = jnp.sum(top_ref[...], axis=1, keepdims=True)
    o_ref[...] = (acc_ref[...] / total).astype(BF)


def causal_attention(queries, near, side, far, q_blocks, k_blocks, rows):
    steps = queries.shape[0] // rows
    whole = lambda a: pl.BlockSpec(a.shape, lambda i, *_: (0, 0))
    return pl.pallas_call(
        causal_kernel,
        grid_spec=pltpu.PrefetchScalarGridSpec(
            num_scalar_prefetch=2,
            grid=(steps,),
            in_specs=[
                pl.BlockSpec((rows, HD), lambda i, *_: (i, 0)),
                whole(near),
                whole(side),
                whole(far),
            ],
            out_specs=pl.BlockSpec((rows, HD), lambda i, *_: (i, 0)),
            scratch_shapes=[
                pltpu.VMEM((16, rows, rows), F32),
                pltpu.VMEM((rows, HD), F32),
                pltpu.VMEM((rows, HD), F32),
            ],
        ),
        out_shape=jax.ShapeDtypeStruct(queries.shape, BF),
        compiler_params=pltpu.CompilerParams(vmem_limit_bytes=14 * 1024 * 1024),
        cost_estimate=LONG,
    )(q_blocks, k_blocks, queries, near, side, far)


def deal_heads(self_queries, self_keys, self_values):
    x = lax.axis_index("ctx") // 4

    def head(k):
        col = (x + k) % NX * HD
        return jnp.concatenate(
            [lax.dynamic_slice_in_dim(a, col, HD, 1) for a in (self_queries, self_keys, self_values)], axis=1
        )

    return [head(0)] + [along_x(head(k), k) for k in (1, 2, 3)]


def near_attention(pieces, near, side):
    rows = pieces[0].shape[0]
    ctx = lax.axis_index("ctx")
    x, rest = ctx // 4, ctx % 4
    queries = jnp.concatenate([p[:, :HD] for p in pieces], axis=0)
    far = swap_rest(jnp.concatenate([near, side], axis=0), 1)
    source_x = jnp.stack([(x - k) % NX for k in range(4)]).astype(jnp.int32)
    q_blocks = source_x * 4 + rest
    k_blocks = jnp.concatenate([source_x * 4 + (rest ^ bits) for bits in (0, 2, 1, 3)])
    return causal_attention(queries, near, side, far, q_blocks, k_blocks, rows)


def return_heads(context):
    x = lax.axis_index("ctx") // 4
    rows = context.shape[0] // NX
    back = [context[:rows]] + [along_x(context[k * rows : (k + 1) * rows], -k) for k in (1, 2, 3)]
    result = jnp.zeros((rows, NX * HD), BF)
    for k in range(4):
        result = lax.dynamic_update_slice(result, back[k], (0, (x + k) % NX * HD))
    return result


def query_kernel(order, gain_ref, w_ref, *refs):
    count = 2 * NY
    piece_refs, (out_ref, w_buf, sems) = refs[:-3], refs[-3:]
    width = w_buf.shape[1]
    copies = []
    for k in range(count):
        first = pl.multiple_of(order[k] * width, width)
        copies.append(pltpu.make_async_copy(w_ref.at[pl.ds(first, width)], w_buf.at[k], sems.at[k]))
    for copy in copies:
        copy.start()

    near_ref, far_ref = piece_refs

    def block(k):
        col = k % NY * width
        if k < NY:
            return near_ref[:, col : col + width].astype(F32)
        low = NY * width + col
        return jnp.concatenate([far_ref[:, col : col + width], far_ref[:, low : low + width]], axis=0).astype(F32)

    square = jnp.zeros((out_ref.shape[0], 1), F32)
    for k in range(count):
        values = block(k)
        square = square + jnp.sum(values * values, axis=1, keepdims=True)
    factor = lax.rsqrt(square * (1.0 / (count * width)) + EPS)
    total = jnp.zeros(out_ref.shape, F32)
    for k in range(count):
        normed = (block(k) * factor * gain_ref[pl.ds(order[k], 1), :]).astype(BF)
        copies[k].wait()
        total = total + jnp.dot(normed, w_buf[k], preferred_element_type=F32)
    out_ref[...] = total.astype(BF)


def project_queries(pieces, gain, weight, order):
    rows, width = pieces[0].shape[0], pieces[0].shape[1] // NY
    vmem = pl.BlockSpec(memory_space=pltpu.VMEM)
    return pl.pallas_call(
        query_kernel,
        in_specs=[pl.BlockSpec(memory_space=pltpu.SMEM), vmem, pl.BlockSpec(memory_space=pl.ANY)] + [vmem] * len(pieces),
        out_specs=vmem,
        out_shape=jax.ShapeDtypeStruct((rows, weight.shape[1]), BF),
        scratch_shapes=[
            pltpu.VMEM((2 * NY, width, weight.shape[1]), BF),
            pltpu.SemaphoreType.DMA((2 * NY,)),
        ],
        compiler_params=pltpu.CompilerParams(vmem_limit_bytes=14 * 1024 * 1024),
        cost_estimate=SHORT,
    )(order, gain.astype(F32).reshape(2 * NY, width), weight, *pieces)


def project_rows(n_refs, w_ref, n_buf, w_buf, acc, n_sems, w_sems):
    deep = w_buf.shape[1]
    copies, first = [], 0
    for i, ref in enumerate(n_refs):
        copies.append(pltpu.make_async_copy(ref, n_buf.at[pl.ds(first, ref.shape[0])], n_sems.at[i]))
        first += ref.shape[0]
    w_copies = [
        pltpu.make_async_copy(w_ref.at[pl.ds(k * deep, deep)], w_buf.at[k], w_sems.at[k]) for k in range(w_buf.shape[0])
    ]
    for copy in copies + w_copies:
        copy.start()
    for copy in copies:
        copy.wait()
    for k, copy in enumerate(w_copies):
        copy.wait()
        part = jnp.dot(n_buf[:, k * deep : (k + 1) * deep], w_buf[k], preferred_element_type=F32)
        if k == 0:
            acc[...] = part
        else:
            acc[...] += part


def rows_kernel(w_ref, *refs):
    n_refs, (out_ref, *scratch) = refs[:-6], refs[-6:]
    project_rows(n_refs, w_ref, *scratch)
    out_ref[...] = scratch[2][...].astype(BF)


def span_kernel(counts, q_ref, kv_ref, w_ref, *refs):
    n_refs, (out_ref, tail_ref, *scratch) = refs[:-7], refs[-7:]
    project_rows(n_refs, w_ref, *scratch)
    acc = scratch[2]
    queries, keys = q_ref.shape[0], acc.shape[0]
    width = q_ref.shape[1]
    heads = width // HD
    spans = queries // SPAN
    rows = keys // NY
    token_rows = rows // spans
    q_span = lax.broadcasted_iota(jnp.int32, (queries, keys), 0) // SPAN
    column = lax.broadcasted_iota(jnp.int32, (queries, keys), 1)
    k_span = column % rows // token_rows
    k_neighbour = column % token_rows // (token_rows // NEIGH)
    used = jnp.zeros((queries, keys), jnp.int32)
    for i in range(spans):
        used = jnp.where(q_span == i, counts[i], used)
    allowed = (q_span == k_span) & (k_neighbour < used)

    def score(query, key):
        s = lax.dot_general(query, key, (((1,), (1,)), ((), ())), preferred_element_type=F32)
        return jnp.where(allowed, s * (1.0 / math.sqrt(HD)), -1e30)

    for h in range(heads):
        cols = slice(h * HD, (h + 1) * HD)
        value_cols = slice(width + h * HD, width + (h + 1) * HD)
        query = q_ref[:, cols]
        first, second = score(query, kv_ref[:, cols]), score(query, acc[:, cols].astype(BF))
        top = jnp.max(jnp.maximum(first, second), axis=1, keepdims=True)
        first, second = jnp.exp(first - top), jnp.exp(second - top)
        total = jnp.sum(first + second, axis=1, keepdims=True)
        context = jnp.dot(first.astype(BF), kv_ref[:, value_cols], preferred_element_type=F32)
        context = context + jnp.dot(
            second.astype(BF), acc[:, value_cols].astype(BF), preferred_element_type=F32
        )
        context = (context / total).astype(BF)
        out_ref[:, cols] = context
        tail_ref[:, cols] = context[queries - SPAN :]


def rows_scratch(normed, weight, steps=8):
    key_rows = sum(piece.shape[0] for piece in normed)
    depth, width = weight.shape
    return [
        pltpu.VMEM((key_rows, depth), BF),
        pltpu.VMEM((steps, depth // steps, width), BF),
        pltpu.VMEM((key_rows, width), F32),
        pltpu.SemaphoreType.DMA((len(normed),)),
        pltpu.SemaphoreType.DMA((steps,)),
    ]


def keys_values(weight, normed):
    any_space = pl.BlockSpec(memory_space=pl.ANY)
    key_rows = sum(piece.shape[0] for piece in normed)
    return pl.pallas_call(
        rows_kernel,
        in_specs=[any_space] * (1 + len(normed)),
        out_specs=pl.BlockSpec(memory_space=pltpu.VMEM),
        out_shape=jax.ShapeDtypeStruct((key_rows, weight.shape[1]), BF),
        scratch_shapes=rows_scratch(normed, weight),
        compiler_params=pltpu.CompilerParams(vmem_limit_bytes=20 * 1024 * 1024),
        cost_estimate=LONG,
    )(weight, *normed)


def attend_spans(queries, counts, kv, weight, normed):
    rows, width = queries.shape
    any_space = pl.BlockSpec(memory_space=pl.ANY)
    vmem = pl.BlockSpec(memory_space=pltpu.VMEM)
    return pl.pallas_call(
        span_kernel,
        in_specs=[pl.BlockSpec(memory_space=pltpu.SMEM), vmem, vmem] + [any_space] * (1 + len(normed)),
        out_specs=(vmem, vmem),
        out_shape=(jax.ShapeDtypeStruct((rows, width), BF), jax.ShapeDtypeStruct((SPAN, width), BF)),
        scratch_shapes=rows_scratch(normed, weight),
        compiler_params=pltpu.CompilerParams(vmem_limit_bytes=20 * 1024 * 1024),
        cost_estimate=SHORT,
    )(counts, queries, kv, weight, *normed)


def split_z(rows):
    z = lax.axis_index("enc") % 2
    part = rows.shape[1] // (2 * NY)

    def take(zz):
        parts = [lax.dynamic_slice_in_dim(rows, (yy * 2 + zz) * part, part, 1) for yy in range(NY)]
        return jnp.concatenate(parts, axis=1)

    return take(z), take(1 - z).astype(BF)


def scatter_sum(top, low, low_far):
    enc = lax.axis_index("enc")
    y, z = enc // 2, enc % 2
    part = low_far.shape[1] // NY

    def pair(a, k):
        return lax.dynamic_slice_in_dim(a, (y + k) % NY * 2 * part, 2 * part, 1)

    low_got = swap_z_hi(low_far)
    top_got = [along_y(pair(top, k).astype(BF), k) for k in (1, 3, 2)]
    low_sum = low + low_got.astype(F32)

    def column(k):
        return lax.dynamic_slice_in_dim(low_sum, (y + k) % NY * part, part, 1)

    last_got = [along_y(column(k).astype(BF), k) for k in (1, 3, 2)]
    top_sum = pair(top, 0)
    for got in top_got:
        top_sum = top_sum + got.astype(F32)
    far = lax.dynamic_slice_in_dim(top_sum, (1 - z) * part, part, 1)
    near = lax.dynamic_slice_in_dim(top_sum, z * part, part, 1)
    top_out = near + swap_z_hi(far.astype(BF)).astype(F32)
    low_out = column(0)
    for got in last_got:
        low_out = low_out + got.astype(F32)
    return jnp.concatenate([top_out, low_out], axis=0)


def per_device(
    self_queries,
    self_keys,
    self_values,
    hidden_in,
    query_gain,
    store_gain,
    store_table,
    cross_query_weight,
    cross_kv_weight,
    self_out_weight,
    cross_out_weight,
    neighbour_ids,
    neighbour_counts,
):
    rows, local_width = self_queries.shape
    enc = lax.axis_index("enc")
    y, z = enc // 2, enc % 2

    request, destination = ask(neighbour_ids.reshape(-1), store_table.shape[0])
    asked = lax.all_to_all(request, ("enc", "ctx"), split_axis=0, concat_axis=0, tiled=True).reshape(-1)
    dealt = deal_heads(*after((self_queries, self_keys, self_values), request))
    near = jnp.concatenate([p[:, HD:] for p in dealt], axis=0)
    found = lookup(after(asked, near), store_table)
    near, hidden, cross_kv_weight = after((near, hidden_in, cross_kv_weight), found)
    side = swap_rest(near, 2)
    hidden = [hidden, along_y(hidden, -1), along_y(hidden, 2), along_y(hidden, 1)]
    kv_weight = cross_kv_weight.reshape(-1, 2 * local_width)

    own_rows = rms_norm(answer(found, destination), store_gain)
    own_rows = after(own_rows, kv_weight, side, *hidden)
    near, side, hidden = after((near, side, hidden), own_rows)
    near_context = near_attention(dealt, near, side)
    self_context = return_heads(near_context)
    hidden = jnp.concatenate(hidden, axis=1)
    folded = jnp.concatenate([hidden[: rows // 2], hidden[rows // 2 :]], axis=1)
    normed, side_normed, far_hidden = gather_rows(own_rows, folded, self_context)
    kv = keys_values(kv_weight, normed)
    self_context = after(self_context, side_normed[2])
    self_projected = jnp.dot(self_context, self_out_weight, preferred_element_type=F32)

    turn = jnp.stack([(y + k) % NY for k in range(NY)]).astype(jnp.int32)
    hidden_order = jnp.concatenate([turn * 2 + z, turn * 2 + 1 - z])
    cross_queries = project_queries([hidden, far_hidden], query_gain, cross_query_weight, hidden_order)
    later = next_ctx(cross_queries[:SPAN], -1)
    queries = jnp.concatenate([cross_queries[SPAN - 1 :], later[: SPAN - 1]], axis=0)

    counts = neighbour_counts.astype(jnp.int32)
    queries = after(queries, kv, self_projected)
    context, tail = attend_spans(queries, counts, kv, kv_weight, side_normed)
    earlier = next_ctx(tail, 1)
    half = rows // 2
    low = self_projected[half:] + jnp.dot(
        context[half - SPAN + 1 : rows - SPAN + 1], cross_out_weight, preferred_element_type=F32
    )
    low, low_far = split_z(low)
    cross_context = jnp.concatenate([earlier[1:], after(context, low_far)[: half - SPAN + 1]], axis=0)
    top = self_projected[:half] + jnp.dot(cross_context, cross_out_weight, preferred_element_type=F32)
    return (hidden_in.astype(F32) + scatter_sum(top, low, low_far)).astype(BF)


def solution(mesh):
    placed = (
        P("ctx", "enc"),
        P("ctx", "enc"),
        P("ctx", "enc"),
        P("ctx", "enc"),
        P(),
        P(),
        P(("enc", "ctx"), None),
        P(None, "enc"),
        P(None, None, "enc"),
        P("enc", None),
        P("enc", None),
        P("ctx", None, "enc"),
        P("ctx"),
    )
    return jax.shard_map(
        per_device, mesh=mesh, in_specs=placed, out_specs=P("ctx", "enc"), check_vma=False
    )
```

```python
import functools
import math

import jax
import jax.numpy as jnp
from jax import lax
from jax.experimental import pallas as pl
from jax.experimental.pallas import tpu as pltpu
from jax.sharding import PartitionSpec as P

HD = 128
SPAN = 64
NEIGH = 2
NLEN = 128
EPS = 1e-06

NY = 4
NX = 4
BF = jnp.bfloat16
F32 = jnp.float32
SHORT = pl.CostEstimate(flops=1024, bytes_accessed=1024, transcendentals=0)
LONG = pl.CostEstimate(flops=1 << 36, bytes_accessed=1 << 28, transcendentals=0)


def along_y(block, step):
    route = [(y * 2 + z, (y + step) % NY * 2 + z) for y in range(NY) for z in range(2)]
    return lax.ppermute(block, "enc", route)


def swap_z_hi(block):
    return lax.ppermute(block, "enc", [(e, e ^ 1) for e in range(2 * NY)])


def along_x(block, step):
    route = [(x * 4 + r, (x + step) % NX * 4 + r) for x in range(NX) for r in range(4)]
    return lax.ppermute(block, "ctx", route)


def swap_rest(block, bits):
    return lax.ppermute(block, "ctx", [(c, c ^ bits) for c in range(4 * NX)])


def next_ctx(block, step):
    size = 4 * NX
    route = [(c, c + step) for c in range(size) if 0 <= c + step < size]
    return lax.ppermute(block, "ctx", route)


def after(values, *done):
    return jax.tree.map(lambda value: lax.optimization_barrier((value, *done))[0], values)


def gather_rows(block, fellow, done):
    half = block.shape[0] // 2
    above, below = along_y(block, -1), along_y(block, 1)
    swapped = swap_z_hi(jnp.concatenate([block, fellow], axis=0))
    side = swapped[: 2 * half]
    onward = after((below, above), done)
    far = along_y(onward[0][:half], 1), along_y(onward[1][half:], -1)
    far = jnp.concatenate(far, axis=0)
    side_above, side_below = along_y(side, -1), along_y(side, 1)
    return (block, above, far, below), (side, side_above, swap_z_hi(far), side_below), swapped[2 * half :]


def rms_norm(rows, gain):
    values = rows.astype(F32)
    factor = lax.rsqrt(jnp.mean(values * values, axis=-1, keepdims=True) + EPS)
    return (values * factor * gain.astype(F32)).astype(BF)


def ask(wanted, shard_rows):
    device_count = lax.axis_size("enc") * lax.axis_size("ctx")
    count = wanted.shape[0]
    owner = wanted // shard_rows
    local_row = wanted - owner * shard_rows
    order = jnp.arange(count, dtype=jnp.int32)
    same = (owner[:, None] == owner[None, :]) & (order[None, :] < order[:, None])
    slot = jnp.sum(same.astype(jnp.int32), axis=1)
    destination = owner * 2 + slot
    place = destination[:, None] == jnp.arange(device_count * 2, dtype=jnp.int32)[None, :]
    buffer = jnp.sum(jnp.where(place, local_row[:, None], 0), axis=0)
    return buffer.reshape(device_count, 2), destination


def lookup(asked, store_table):
    return store_table.reshape(-1, store_table.shape[1] // HD, HD)[asked]


def answer(found, destination):
    came = lax.all_to_all(found, ("enc", "ctx"), split_axis=0, concat_axis=0, tiled=True)
    return came[destination].reshape(destination.shape[0], -1)


def causal_kernel(q_blocks, k_blocks, q_ref, near_ref, side_ref, far_ref, o_ref, s_ref, top_ref, acc_ref):
    rows = q_ref.shape[0]
    step = pl.program_id(0)
    mine = q_blocks[step]
    scale = 1.0 / math.sqrt(HD)
    query = q_ref[...]
    parts = [(near_ref, i) for i in range(4)] + [(side_ref, i) for i in range(4)]
    parts = parts + [(far_ref, i) for i in range(8)]
    top_ref[...] = jnp.full(top_ref.shape, -1e30, F32)
    for j, (ref, i) in enumerate(parts):
        @pl.when(k_blocks[j] <= mine)
        def _(j=j, ref=ref, i=i):
            key = ref[i * rows : (i + 1) * rows, :HD]
            s = lax.dot_general(query, key, (((1,), (1,)), ((), ())), preferred_element_type=F32) * scale
            offset = jnp.where(k_blocks[j] == mine, 0, rows)
            q_pos = lax.broadcasted_iota(jnp.int32, s.shape, 0) + offset
            k_pos = lax.broadcasted_iota(jnp.int32, s.shape, 1)
            s = jnp.where(q_pos >= k_pos, s, -1e30)
            s_ref[j] = s
            best = top_ref[...]
            for part in range(rows // HD):
                best = jnp.maximum(best, s[:, part * HD : (part + 1) * HD])
            top_ref[...] = best
    top = jnp.max(top_ref[...], axis=1, keepdims=True)
    acc_ref[...] = jnp.zeros(acc_ref.shape, F32)
    top_ref[...] = jnp.zeros(top_ref.shape, F32)
    for j, (ref, i) in enumerate(parts):
        @pl.when(k_blocks[j] <= mine)
        def _(j=j, ref=ref, i=i):
            value = ref[i * rows : (i + 1) * rows, HD:]
            w = jnp.exp(s_ref[j] - top)
            total = top_ref[...]
            for part in range(rows // HD):
                total = total + w[:, part * HD : (part + 1) * HD]
            top_ref[...] = total
            acc_ref[...] += jnp.dot(w.astype(BF), value, preferred_element_type=F32)
    total = jnp.sum(top_ref[...], axis=1, keepdims=True)
    o_ref[...] = (acc_ref[...] / total).astype(BF)


def causal_attention(queries, near, side, far, q_blocks, k_blocks, rows):
    steps = queries.shape[0] // rows
    whole = lambda a: pl.BlockSpec(a.shape, lambda i, *_: (0, 0))
    return pl.pallas_call(
        causal_kernel,
        grid_spec=pltpu.PrefetchScalarGridSpec(
            num_scalar_prefetch=2,
            grid=(steps,),
            in_specs=[
                pl.BlockSpec((rows, HD), lambda i, *_: (i, 0)),
                whole(near),
                whole(side),
                whole(far),
            ],
            out_specs=pl.BlockSpec((rows, HD), lambda i, *_: (i, 0)),
            scratch_shapes=[
                pltpu.VMEM((16, rows, rows), F32),
                pltpu.VMEM((rows, HD), F32),
                pltpu.VMEM((rows, HD), F32),
            ],
        ),
        out_shape=jax.ShapeDtypeStruct(queries.shape, BF),
        compiler_params=pltpu.CompilerParams(vmem_limit_bytes=14 * 1024 * 1024),
        cost_estimate=LONG,
    )(q_blocks, k_blocks, queries, near, side, far)


def deal_heads(self_queries, self_keys, self_values):
    x = lax.axis_index("ctx") // 4

    def head(k):
        col = (x + k) % NX * HD
        return jnp.concatenate(
            [lax.dynamic_slice_in_dim(a, col, HD, 1) for a in (self_queries, self_keys, self_values)], axis=1
        )

    return [head(0)] + [along_x(head(k), k) for k in (1, 2, 3)]


def near_attention(pieces, near, side):
    rows = pieces[0].shape[0]
    ctx = lax.axis_index("ctx")
    x, rest = ctx // 4, ctx % 4
    queries = jnp.concatenate([p[:, :HD] for p in pieces], axis=0)
    far = swap_rest(jnp.concatenate([near, side], axis=0), 1)
    source_x = jnp.stack([(x - k) % NX for k in range(4)]).astype(jnp.int32)
    q_blocks = source_x * 4 + rest
    k_blocks = jnp.concatenate([source_x * 4 + (rest ^ bits) for bits in (0, 2, 1, 3)])
    return causal_attention(queries, near, side, far, q_blocks, k_blocks, rows)


def return_heads(context):
    x = lax.axis_index("ctx") // 4
    rows = context.shape[0] // NX
    back = [context[:rows]] + [along_x(context[k * rows : (k + 1) * rows], -k) for k in (1, 2, 3)]
    result = jnp.zeros((rows, NX * HD), BF)
    for k in range(4):
        result = lax.dynamic_update_slice(result, back[k], (0, (x + k) % NX * HD))
    return result


def query_kernel(order, gain_ref, w_ref, *refs):
    count = 2 * NY
    piece_refs, (out_ref, w_buf, sems) = refs[:-3], refs[-3:]
    width = w_buf.shape[1]
    copies = []
    for k in range(count):
        first = pl.multiple_of(order[k] * width, width)
        copies.append(pltpu.make_async_copy(w_ref.at[pl.ds(first, width)], w_buf.at[k], sems.at[k]))
    for copy in copies:
        copy.start()

    near_ref, far_ref = piece_refs

    def block(k):
        col = k % NY * width
        if k < NY:
            return near_ref[:, col : col + width].astype(F32)
        low = NY * width + col
        return jnp.concatenate([far_ref[:, col : col + width], far_ref[:, low : low + width]], axis=0).astype(F32)

    square = jnp.zeros((out_ref.shape[0], 1), F32)
    for k in range(count):
        values = block(k)
        square = square + jnp.sum(values * values, axis=1, keepdims=True)
    factor = lax.rsqrt(square * (1.0 / (count * width)) + EPS)
    total = jnp.zeros(out_ref.shape, F32)
    for k in range(count):
        normed = (block(k) * factor * gain_ref[pl.ds(order[k], 1), :]).astype(BF)
        copies[k].wait()
        total = total + jnp.dot(normed, w_buf[k], preferred_element_type=F32)
    out_ref[...] = total.astype(BF)


def project_queries(pieces, gain, weight, order):
    rows, width = pieces[0].shape[0], pieces[0].shape[1] // NY
    vmem = pl.BlockSpec(memory_space=pltpu.VMEM)
    return pl.pallas_call(
        query_kernel,
        in_specs=[pl.BlockSpec(memory_space=pltpu.SMEM), vmem, pl.BlockSpec(memory_space=pl.ANY)] + [vmem] * len(pieces),
        out_specs=vmem,
        out_shape=jax.ShapeDtypeStruct((rows, weight.shape[1]), BF),
        scratch_shapes=[
            pltpu.VMEM((2 * NY, width, weight.shape[1]), BF),
            pltpu.SemaphoreType.DMA((2 * NY,)),
        ],
        compiler_params=pltpu.CompilerParams(vmem_limit_bytes=14 * 1024 * 1024),
        cost_estimate=SHORT,
    )(order, gain.astype(F32).reshape(2 * NY, width), weight, *pieces)


def project_rows(n_refs, w_ref, n_buf, w_buf, acc, n_sems, w_sems):
    deep = w_buf.shape[1]
    copies, first = [], 0
    for i, ref in enumerate(n_refs):
        copies.append(pltpu.make_async_copy(ref, n_buf.at[pl.ds(first, ref.shape[0])], n_sems.at[i]))
        first += ref.shape[0]
    w_copies = [
        pltpu.make_async_copy(w_ref.at[pl.ds(k * deep, deep)], w_buf.at[k], w_sems.at[k]) for k in range(w_buf.shape[0])
    ]
    for copy in copies + w_copies:
        copy.start()
    for copy in copies:
        copy.wait()
    for k, copy in enumerate(w_copies):
        copy.wait()
        part = jnp.dot(n_buf[:, k * deep : (k + 1) * deep], w_buf[k], preferred_element_type=F32)
        if k == 0:
            acc[...] = part
        else:
            acc[...] += part


def rows_kernel(w_ref, *refs):
    n_refs, (out_ref, *scratch) = refs[:-6], refs[-6:]
    project_rows(n_refs, w_ref, *scratch)
    out_ref[...] = scratch[2][...].astype(BF)


def span_kernel(counts, q_ref, kv_ref, w_ref, *refs):
    n_refs, (out_ref, tail_ref, *scratch) = refs[:-7], refs[-7:]
    project_rows(n_refs, w_ref, *scratch)
    acc = scratch[2]
    queries, keys = q_ref.shape[0], acc.shape[0]
    width = q_ref.shape[1]
    heads = width // HD
    spans = queries // SPAN
    rows = keys // NY
    token_rows = rows // spans
    q_span = lax.broadcasted_iota(jnp.int32, (queries, keys), 0) // SPAN
    column = lax.broadcasted_iota(jnp.int32, (queries, keys), 1)
    k_span = column % rows // token_rows
    k_neighbour = column % token_rows // (token_rows // NEIGH)
    used = jnp.zeros((queries, keys), jnp.int32)
    for i in range(spans):
        used = jnp.where(q_span == i, counts[i], used)
    allowed = (q_span == k_span) & (k_neighbour < used)

    def score(query, key):
        s = lax.dot_general(query, key, (((1,), (1,)), ((), ())), preferred_element_type=F32)
        return jnp.where(allowed, s * (1.0 / math.sqrt(HD)), -1e30)

    for h in range(heads):
        cols = slice(h * HD, (h + 1) * HD)
        value_cols = slice(width + h * HD, width + (h + 1) * HD)
        query = q_ref[:, cols]
        first, second = score(query, kv_ref[:, cols]), score(query, acc[:, cols].astype(BF))
        top = jnp.max(jnp.maximum(first, second), axis=1, keepdims=True)
        first, second = jnp.exp(first - top), jnp.exp(second - top)
        total = jnp.sum(first + second, axis=1, keepdims=True)
        context = jnp.dot(first.astype(BF), kv_ref[:, value_cols], preferred_element_type=F32)
        context = context + jnp.dot(
            second.astype(BF), acc[:, value_cols].astype(BF), preferred_element_type=F32
        )
        context = (context / total).astype(BF)
        out_ref[:, cols] = context
        tail_ref[:, cols] = context[queries - SPAN :]


def rows_scratch(normed, weight, steps=4):
    key_rows = sum(piece.shape[0] for piece in normed)
    depth, width = weight.shape
    return [
        pltpu.VMEM((key_rows, depth), BF),
        pltpu.VMEM((steps, depth // steps, width), BF),
        pltpu.VMEM((key_rows, width), F32),
        pltpu.SemaphoreType.DMA((len(normed),)),
        pltpu.SemaphoreType.DMA((steps,)),
    ]


def keys_values(weight, normed):
    any_space = pl.BlockSpec(memory_space=pl.ANY)
    key_rows = sum(piece.shape[0] for piece in normed)
    return pl.pallas_call(
        rows_kernel,
        in_specs=[any_space] * (1 + len(normed)),
        out_specs=pl.BlockSpec(memory_space=pltpu.VMEM),
        out_shape=jax.ShapeDtypeStruct((key_rows, weight.shape[1]), BF),
        scratch_shapes=rows_scratch(normed, weight),
        compiler_params=pltpu.CompilerParams(vmem_limit_bytes=20 * 1024 * 1024),
        cost_estimate=LONG,
    )(weight, *normed)


def attend_spans(queries, counts, kv, weight, normed):
    rows, width = queries.shape
    any_space = pl.BlockSpec(memory_space=pl.ANY)
    vmem = pl.BlockSpec(memory_space=pltpu.VMEM)
    return pl.pallas_call(
        span_kernel,
        in_specs=[pl.BlockSpec(memory_space=pltpu.SMEM), vmem, vmem] + [any_space] * (1 + len(normed)),
        out_specs=(vmem, vmem),
        out_shape=(jax.ShapeDtypeStruct((rows, width), BF), jax.ShapeDtypeStruct((SPAN, width), BF)),
        scratch_shapes=rows_scratch(normed, weight),
        compiler_params=pltpu.CompilerParams(vmem_limit_bytes=20 * 1024 * 1024),
        cost_estimate=SHORT,
    )(counts, queries, kv, weight, *normed)


def split_z(rows):
    z = lax.axis_index("enc") % 2
    part = rows.shape[1] // (2 * NY)

    def take(zz):
        parts = [lax.dynamic_slice_in_dim(rows, (yy * 2 + zz) * part, part, 1) for yy in range(NY)]
        return jnp.concatenate(parts, axis=1)

    return take(z), take(1 - z).astype(BF)


def scatter_sum(top, low, low_far):
    enc = lax.axis_index("enc")
    y, z = enc // 2, enc % 2
    part = low_far.shape[1] // NY
    low_got = swap_z_hi(low_far)

    def pair(k):
        return lax.dynamic_slice_in_dim(top, (y + k) % NY * 2 * part, 2 * part, 1)

    top_sum, *top_pairs = lax.optimization_barrier([pair(0)] + [pair(k).astype(BF) for k in (1, 3, 2)])
    top_got = [along_y(block, k) for block, k in zip(top_pairs, (1, 3, 2))]
    low_sum = low + low_got.astype(F32)

    def column(k):
        return lax.dynamic_slice_in_dim(low_sum, (y + k) % NY * part, part, 1)

    low_out, *low_parts = lax.optimization_barrier([column(0)] + [column(k).astype(BF) for k in (1, 3, 2)])
    last_got = [along_y(block, k) for block, k in zip(low_parts, (1, 3, 2))]
    top_got = after(top_got, *low_parts)
    for got in top_got:
        top_sum = top_sum + got.astype(F32)
    far = lax.dynamic_slice_in_dim(top_sum, (1 - z) * part, part, 1)
    near = lax.dynamic_slice_in_dim(top_sum, z * part, part, 1)
    top_out = near + swap_z_hi(far.astype(BF)).astype(F32)
    for got in last_got:
        low_out = low_out + got.astype(F32)
    return jnp.concatenate([top_out, low_out], axis=0)


def per_device(
    self_queries,
    self_keys,
    self_values,
    hidden_in,
    query_gain,
    store_gain,
    store_table,
    cross_query_weight,
    cross_kv_weight,
    self_out_weight,
    cross_out_weight,
    neighbour_ids,
    neighbour_counts,
):
    rows, local_width = self_queries.shape
    enc = lax.axis_index("enc")
    y, z = enc // 2, enc % 2

    request, destination = ask(neighbour_ids.reshape(-1), store_table.shape[0])
    asked = lax.all_to_all(request, ("enc", "ctx"), split_axis=0, concat_axis=0, tiled=True).reshape(-1)
    dealt = deal_heads(*after((self_queries, self_keys, self_values), request))
    near = jnp.concatenate([p[:, HD:] for p in dealt], axis=0)
    found = lookup(after(asked, near), store_table)
    near, hidden, cross_kv_weight = after((near, hidden_in, cross_kv_weight), found)
    side = swap_rest(near, 2)
    hidden = [hidden, along_y(hidden, -1), along_y(hidden, 2), along_y(hidden, 1)]
    kv_weight = cross_kv_weight.reshape(-1, 2 * local_width)

    own_rows = rms_norm(answer(found, destination), store_gain)
    own_rows = after(own_rows, kv_weight, side, *hidden)
    near, side, hidden = after((near, side, hidden), own_rows)
    near_context = near_attention(dealt, near, side)
    self_context = return_heads(near_context)
    hidden = jnp.concatenate(hidden, axis=1)
    folded = jnp.concatenate([hidden[: rows // 2], hidden[rows // 2 :]], axis=1)
    normed, side_normed, far_hidden = gather_rows(own_rows, folded, self_context)
    kv = keys_values(kv_weight, normed)
    self_context = after(self_context, side_normed[2])
    self_projected = jnp.dot(self_context, self_out_weight, preferred_element_type=F32)

    turn = jnp.stack([(y + k) % NY for k in range(NY)]).astype(jnp.int32)
    hidden_order = jnp.concatenate([turn * 2 + z, turn * 2 + 1 - z])
    cross_queries = project_queries([hidden, far_hidden], query_gain, cross_query_weight, hidden_order)
    later = next_ctx(cross_queries[:SPAN], -1)
    queries = jnp.concatenate([cross_queries[SPAN - 1 :], later[: SPAN - 1]], axis=0)

    counts = neighbour_counts.astype(jnp.int32)
    queries = after(queries, kv, self_projected)
    context, tail = attend_spans(queries, counts, kv, kv_weight, side_normed)
    earlier = next_ctx(tail, 1)
    half = rows // 2
    low = self_projected[half:] + jnp.dot(
        context[half - SPAN + 1 : rows - SPAN + 1], cross_out_weight, preferred_element_type=F32
    )
    low, low_far = split_z(low)
    cross_context = jnp.concatenate([earlier[1:], after(context, low_far)[: half - SPAN + 1]], axis=0)
    top = self_projected[:half] + jnp.dot(cross_context, cross_out_weight, preferred_element_type=F32)
    return (hidden_in.astype(F32) + scatter_sum(top, low, low_far)).astype(BF)


def solution(mesh):
    placed = (
        P("ctx", "enc"),
        P("ctx", "enc"),
        P("ctx", "enc"),
        P("ctx", "enc"),
        P(),
        P(),
        P(("enc", "ctx"), None),
        P(None, "enc"),
        P(None, None, "enc"),
        P("enc", None),
        P("enc", None),
        P("ctx", None, "enc"),
        P("ctx"),
    )
    return jax.shard_map(
        per_device, mesh=mesh, in_specs=placed, out_specs=P("ctx", "enc"), check_vma=False
    )
```

```python
import functools
import math

import jax
import jax.numpy as jnp
from jax import lax
from jax.experimental import pallas as pl
from jax.experimental.pallas import tpu as pltpu
from jax.sharding import PartitionSpec as P

HD = 128
SPAN = 64
NEIGH = 2
NLEN = 128
EPS = 1e-06

NY = 4
NX = 4
BF = jnp.bfloat16
F32 = jnp.float32
SHORT = pl.CostEstimate(flops=1024, bytes_accessed=1024, transcendentals=0)
LONG = pl.CostEstimate(flops=1 << 36, bytes_accessed=1 << 28, transcendentals=0)


def along_y(block, step):
    route = [(y * 2 + z, (y + step) % NY * 2 + z) for y in range(NY) for z in range(2)]
    return lax.ppermute(block, "enc", route)


def swap_z_hi(block):
    return lax.ppermute(block, "enc", [(e, e ^ 1) for e in range(2 * NY)])


def along_x(block, step):
    route = [(x * 4 + r, (x + step) % NX * 4 + r) for x in range(NX) for r in range(4)]
    return lax.ppermute(block, "ctx", route)


def swap_rest(block, bits):
    return lax.ppermute(block, "ctx", [(c, c ^ bits) for c in range(4 * NX)])


def next_ctx(block, step):
    size = 4 * NX
    route = [(c, c + step) for c in range(size) if 0 <= c + step < size]
    return lax.ppermute(block, "ctx", route)


def after(values, *done):
    return jax.tree.map(lambda value: lax.optimization_barrier((value, *done))[0], values)


def gather_rows(block, fellow, done):
    half = block.shape[0] // 2
    above, below = along_y(block, -1), along_y(block, 1)
    swapped = swap_z_hi(jnp.concatenate([block, fellow], axis=0))
    side = swapped[: 2 * half]
    onward = after((below, above), done)
    far = along_y(onward[0][:half], 1), along_y(onward[1][half:], -1)
    far = jnp.concatenate(far, axis=0)
    side_above, side_below = along_y(side, -1), along_y(side, 1)
    return (block, above, far, below), (side, side_above, swap_z_hi(far), side_below), swapped


def rms_norm(rows, gain):
    values = rows.astype(F32)
    factor = lax.rsqrt(jnp.mean(values * values, axis=-1, keepdims=True) + EPS)
    return (values * factor * gain.astype(F32)).astype(BF)


def ask(wanted, shard_rows):
    device_count = lax.axis_size("enc") * lax.axis_size("ctx")
    count = wanted.shape[0]
    owner = wanted // shard_rows
    local_row = wanted - owner * shard_rows
    order = jnp.arange(count, dtype=jnp.int32)
    same = (owner[:, None] == owner[None, :]) & (order[None, :] < order[:, None])
    slot = jnp.sum(same.astype(jnp.int32), axis=1)
    destination = owner * 2 + slot
    place = destination[:, None] == jnp.arange(device_count * 2, dtype=jnp.int32)[None, :]
    buffer = jnp.sum(jnp.where(place, local_row[:, None], 0), axis=0)
    return buffer.reshape(device_count, 2), destination


def lookup(asked, store_table):
    return store_table.reshape(-1, store_table.shape[1] // HD, HD)[asked]


def answer(found, destination):
    came = lax.all_to_all(found, ("enc", "ctx"), split_axis=0, concat_axis=0, tiled=True)
    return came[destination].reshape(destination.shape[0], -1)


def causal_kernel(q_blocks, k_blocks, q_ref, near_ref, side_ref, far_ref, o_ref, s_ref, top_ref, acc_ref):
    rows = q_ref.shape[0]
    step = pl.program_id(0)
    mine = q_blocks[step]
    scale = 1.0 / math.sqrt(HD)
    query = q_ref[...]
    parts = [(near_ref, i) for i in range(4)] + [(side_ref, i) for i in range(4)]
    parts = parts + [(far_ref, i) for i in range(8)]
    top_ref[...] = jnp.full(top_ref.shape, -1e30, F32)
    for j, (ref, i) in enumerate(parts):
        @pl.when(k_blocks[j] <= mine)
        def _(j=j, ref=ref, i=i):
            key = ref[i * rows : (i + 1) * rows, :HD]
            s = lax.dot_general(query, key, (((1,), (1,)), ((), ())), preferred_element_type=F32) * scale
            offset = jnp.where(k_blocks[j] == mine, 0, rows)
            q_pos = lax.broadcasted_iota(jnp.int32, s.shape, 0) + offset
            k_pos = lax.broadcasted_iota(jnp.int32, s.shape, 1)
            s = jnp.where(q_pos >= k_pos, s, -1e30)
            s_ref[j] = s
            best = top_ref[...]
            for part in range(rows // HD):
                best = jnp.maximum(best, s[:, part * HD : (part + 1) * HD])
            top_ref[...] = best
    top = jnp.max(top_ref[...], axis=1, keepdims=True)
    acc_ref[...] = jnp.zeros(acc_ref.shape, F32)
    top_ref[...] = jnp.zeros(top_ref.shape, F32)
    for j, (ref, i) in enumerate(parts):
        @pl.when(k_blocks[j] <= mine)
        def _(j=j, ref=ref, i=i):
            value = ref[i * rows : (i + 1) * rows, HD:]
            w = jnp.exp(s_ref[j] - top)
            total = top_ref[...]
            for part in range(rows // HD):
                total = total + w[:, part * HD : (part + 1) * HD]
            top_ref[...] = total
            acc_ref[...] += jnp.dot(w.astype(BF), value, preferred_element_type=F32)
    total = jnp.sum(top_ref[...], axis=1, keepdims=True)
    o_ref[...] = (acc_ref[...] / total).astype(BF)


def causal_attention(queries, near, side, far, q_blocks, k_blocks, rows):
    steps = queries.shape[0] // rows
    whole = lambda a: pl.BlockSpec(a.shape, lambda i, *_: (0, 0))
    return pl.pallas_call(
        causal_kernel,
        grid_spec=pltpu.PrefetchScalarGridSpec(
            num_scalar_prefetch=2,
            grid=(steps,),
            in_specs=[
                pl.BlockSpec((rows, HD), lambda i, *_: (i, 0)),
                whole(near),
                whole(side),
                whole(far),
            ],
            out_specs=pl.BlockSpec((rows, HD), lambda i, *_: (i, 0)),
            scratch_shapes=[
                pltpu.VMEM((16, rows, rows), F32),
                pltpu.VMEM((rows, HD), F32),
                pltpu.VMEM((rows, HD), F32),
            ],
        ),
        out_shape=jax.ShapeDtypeStruct(queries.shape, BF),
        compiler_params=pltpu.CompilerParams(vmem_limit_bytes=14 * 1024 * 1024),
        cost_estimate=LONG,
    )(q_blocks, k_blocks, queries, near, side, far)


def deal_heads(self_queries, self_keys, self_values):
    x = lax.axis_index("ctx") // 4

    def head(k):
        col = (x + k) % NX * HD
        return jnp.concatenate(
            [lax.dynamic_slice_in_dim(a, col, HD, 1) for a in (self_queries, self_keys, self_values)], axis=1
        )

    return [head(0)] + [along_x(head(k), k) for k in (1, 2, 3)]


def near_attention(queries, near, side):
    rows = queries.shape[0] // NX
    ctx = lax.axis_index("ctx")
    x, rest = ctx // 4, ctx % 4
    far = swap_rest(jnp.concatenate([near, side], axis=0), 1)
    source_x = jnp.stack([(x - k) % NX for k in range(4)]).astype(jnp.int32)
    q_blocks = source_x * 4 + rest
    k_blocks = jnp.concatenate([source_x * 4 + (rest ^ bits) for bits in (0, 2, 1, 3)])
    return causal_attention(queries, near, side, far, q_blocks, k_blocks, rows)


def return_heads(context):
    x = lax.axis_index("ctx") // 4
    rows = context.shape[0] // NX
    back = [context[:rows]] + [along_x(context[k * rows : (k + 1) * rows], -k) for k in (1, 2, 3)]
    result = jnp.zeros((rows, NX * HD), BF)
    for k in range(4):
        result = lax.dynamic_update_slice(result, back[k], (0, (x + k) % NX * HD))
    return result


def query_kernel(order, gain_ref, w_ref, *refs):
    count = 2 * NY
    piece_refs, (out_ref, w_buf, sems) = refs[:-3], refs[-3:]
    width = w_buf.shape[1]
    copies = []
    for k in range(count):
        first = pl.multiple_of(order[k] * width, width)
        copies.append(pltpu.make_async_copy(w_ref.at[pl.ds(first, width)], w_buf.at[k], sems.at[k]))
    for copy in copies:
        copy.start()

    near_ref, far_ref = piece_refs

    def block(k):
        col = k % NY * width
        if k < NY:
            return near_ref[:, col : col + width].astype(F32)
        low, first = NY * width + col, far_ref.shape[0] // 2
        parts = [far_ref[first:, col : col + width], far_ref[first:, low : low + width]]
        return jnp.concatenate(parts, axis=0).astype(F32)

    square = jnp.zeros((out_ref.shape[0], 1), F32)
    for k in range(count):
        values = block(k)
        square = square + jnp.sum(values * values, axis=1, keepdims=True)
    factor = lax.rsqrt(square * (1.0 / (count * width)) + EPS)
    total = jnp.zeros(out_ref.shape, F32)
    for k in range(count):
        normed = (block(k) * factor * gain_ref[pl.ds(order[k], 1), :]).astype(BF)
        copies[k].wait()
        total = total + jnp.dot(normed, w_buf[k], preferred_element_type=F32)
    out_ref[...] = total.astype(BF)


def project_queries(pieces, gain, weight, order):
    rows, width = pieces[0].shape[0], pieces[0].shape[1] // NY
    vmem = pl.BlockSpec(memory_space=pltpu.VMEM)
    return pl.pallas_call(
        query_kernel,
        in_specs=[pl.BlockSpec(memory_space=pltpu.SMEM), vmem, pl.BlockSpec(memory_space=pl.ANY)] + [vmem] * len(pieces),
        out_specs=vmem,
        out_shape=jax.ShapeDtypeStruct((rows, weight.shape[1]), BF),
        scratch_shapes=[
            pltpu.VMEM((2 * NY, width, weight.shape[1]), BF),
            pltpu.SemaphoreType.DMA((2 * NY,)),
        ],
        compiler_params=pltpu.CompilerParams(vmem_limit_bytes=14 * 1024 * 1024),
        cost_estimate=SHORT,
    )(order, gain.astype(F32).reshape(2 * NY, width), weight, *pieces)


def project_rows(n_refs, w_ref, n_buf, w_buf, acc, n_sems, w_sems):
    deep = w_buf.shape[1]
    copies, first = [], 0
    for i, ref in enumerate(n_refs):
        copies.append(pltpu.make_async_copy(ref, n_buf.at[pl.ds(first, ref.shape[0])], n_sems.at[i]))
        first += ref.shape[0]
    w_copies = [
        pltpu.make_async_copy(w_ref.at[pl.ds(k * deep, deep)], w_buf.at[k], w_sems.at[k]) for k in range(w_buf.shape[0])
    ]
    for copy in copies + w_copies:
        copy.start()
    for copy in copies:
        copy.wait()
    for k, copy in enumerate(w_copies):
        copy.wait()
        part = jnp.dot(n_buf[:, k * deep : (k + 1) * deep], w_buf[k], preferred_element_type=F32)
        if k == 0:
            acc[...] = part
        else:
            acc[...] += part


def rows_kernel(w_ref, *refs):
    n_refs, (out_ref, *scratch) = refs[:-6], refs[-6:]
    project_rows(n_refs, w_ref, *scratch)
    out_ref[...] = scratch[2][...].astype(BF)


def span_kernel(counts, q_ref, kv_ref, w_ref, *refs):
    n_refs, (out_ref, tail_ref, *scratch) = refs[:-7], refs[-7:]
    project_rows(n_refs, w_ref, *scratch)
    acc = scratch[2]
    queries, keys = q_ref.shape[0], acc.shape[0]
    width = q_ref.shape[1]
    heads = width // HD
    spans = queries // SPAN
    rows = keys // NY
    token_rows = rows // spans
    q_span = lax.broadcasted_iota(jnp.int32, (queries, keys), 0) // SPAN
    column = lax.broadcasted_iota(jnp.int32, (queries, keys), 1)
    k_span = column % rows // token_rows
    k_neighbour = column % token_rows // (token_rows // NEIGH)
    used = jnp.zeros((queries, keys), jnp.int32)
    for i in range(spans):
        used = jnp.where(q_span == i, counts[i], used)
    allowed = (q_span == k_span) & (k_neighbour < used)

    def score(query, key):
        s = lax.dot_general(query, key, (((1,), (1,)), ((), ())), preferred_element_type=F32)
        return jnp.where(allowed, s * (1.0 / math.sqrt(HD)), -1e30)

    for h in range(heads):
        cols = slice(h * HD, (h + 1) * HD)
        value_cols = slice(width + h * HD, width + (h + 1) * HD)
        query = q_ref[:, cols]
        first, second = score(query, kv_ref[:, cols]), score(query, acc[:, cols].astype(BF))
        top = jnp.max(jnp.maximum(first, second), axis=1, keepdims=True)
        first, second = jnp.exp(first - top), jnp.exp(second - top)
        total = jnp.sum(first + second, axis=1, keepdims=True)
        context = jnp.dot(first.astype(BF), kv_ref[:, value_cols], preferred_element_type=F32)
        context = context + jnp.dot(
            second.astype(BF), acc[:, value_cols].astype(BF), preferred_element_type=F32
        )
        context = (context / total).astype(BF)
        out_ref[:, cols] = context
        tail_ref[:, cols] = context[queries - SPAN :]


def rows_scratch(normed, weight, steps=4):
    key_rows = sum(piece.shape[0] for piece in normed)
    depth, width = weight.shape
    return [
        pltpu.VMEM((key_rows, depth), BF),
        pltpu.VMEM((steps, depth // steps, width), BF),
        pltpu.VMEM((key_rows, width), F32),
        pltpu.SemaphoreType.DMA((len(normed),)),
        pltpu.SemaphoreType.DMA((steps,)),
    ]


def keys_values(weight, normed):
    any_space = pl.BlockSpec(memory_space=pl.ANY)
    key_rows = sum(piece.shape[0] for piece in normed)
    return pl.pallas_call(
        rows_kernel,
        in_specs=[any_space] * (1 + len(normed)),
        out_specs=pl.BlockSpec(memory_space=pltpu.VMEM),
        out_shape=jax.ShapeDtypeStruct((key_rows, weight.shape[1]), BF),
        scratch_shapes=rows_scratch(normed, weight),
        compiler_params=pltpu.CompilerParams(vmem_limit_bytes=20 * 1024 * 1024),
        cost_estimate=LONG,
    )(weight, *normed)


def attend_spans(queries, counts, kv, weight, normed):
    rows, width = queries.shape
    any_space = pl.BlockSpec(memory_space=pl.ANY)
    vmem = pl.BlockSpec(memory_space=pltpu.VMEM)
    return pl.pallas_call(
        span_kernel,
        in_specs=[pl.BlockSpec(memory_space=pltpu.SMEM), vmem, vmem] + [any_space] * (1 + len(normed)),
        out_specs=(vmem, vmem),
        out_shape=(jax.ShapeDtypeStruct((rows, width), BF), jax.ShapeDtypeStruct((SPAN, width), BF)),
        scratch_shapes=rows_scratch(normed, weight),
        compiler_params=pltpu.CompilerParams(vmem_limit_bytes=20 * 1024 * 1024),
        cost_estimate=SHORT,
    )(counts, queries, kv, weight, *normed)


def split_z(rows):
    z = lax.axis_index("enc") % 2
    part = rows.shape[1] // (2 * NY)

    def take(zz):
        parts = [lax.dynamic_slice_in_dim(rows, (yy * 2 + zz) * part, part, 1) for yy in range(NY)]
        return jnp.concatenate(parts, axis=1)

    return take(z), take(1 - z).astype(BF)


def scatter_sum(top, low, low_far):
    enc = lax.axis_index("enc")
    y, z = enc // 2, enc % 2
    part = low_far.shape[1] // NY
    low_got = swap_z_hi(low_far)

    def pair(k):
        return lax.dynamic_slice_in_dim(top, (y + k) % NY * 2 * part, 2 * part, 1)

    top_sum, *top_pairs = lax.optimization_barrier([pair(0)] + [pair(k).astype(BF) for k in (1, 3, 2)])
    top_got = [along_y(block, k) for block, k in zip(top_pairs, (1, 3, 2))]
    low_sum = low + low_got.astype(F32)

    def column(k):
        return lax.dynamic_slice_in_dim(low_sum, (y + k) % NY * part, part, 1)

    low_out, *low_parts = lax.optimization_barrier([column(0)] + [column(k).astype(BF) for k in (1, 3, 2)])
    last_got = [along_y(block, k) for block, k in zip(low_parts, (1, 3, 2))]
    top_got = after(top_got, *low_parts)
    for got in top_got:
        top_sum = top_sum + got.astype(F32)
    far = lax.dynamic_slice_in_dim(top_sum, (1 - z) * part, part, 1)
    near = lax.dynamic_slice_in_dim(top_sum, z * part, part, 1)
    top_out = near + swap_z_hi(far.astype(BF)).astype(F32)
    for got in last_got:
        low_out = low_out + got.astype(F32)
    return jnp.concatenate([top_out, low_out], axis=0)


def per_device(
    self_queries,
    self_keys,
    self_values,
    hidden_in,
    query_gain,
    store_gain,
    store_table,
    cross_query_weight,
    cross_kv_weight,
    self_out_weight,
    cross_out_weight,
    neighbour_ids,
    neighbour_counts,
):
    rows, local_width = self_queries.shape
    enc = lax.axis_index("enc")
    y, z = enc // 2, enc % 2

    request, destination = ask(neighbour_ids.reshape(-1), store_table.shape[0])
    asked = lax.all_to_all(request, ("enc", "ctx"), split_axis=0, concat_axis=0, tiled=True).reshape(-1)
    dealt = deal_heads(*after((self_queries, self_keys, self_values), request))
    near = jnp.concatenate([p[:, HD:] for p in dealt], axis=0)
    dealt = jnp.concatenate([p[:, :HD] for p in dealt], axis=0)
    found = lookup(after(asked, near), store_table)
    near, hidden, cross_kv_weight = after((near, hidden_in, cross_kv_weight), found)
    side = swap_rest(near, 2)
    hidden = [hidden, along_y(hidden, -1), along_y(hidden, 2), along_y(hidden, 1)]
    kv_weight = cross_kv_weight.reshape(-1, 2 * local_width)

    own_rows = rms_norm(answer(found, destination), store_gain)
    own_rows = after(own_rows, kv_weight, side, dealt, *hidden)
    near, side, hidden = after((near, side, hidden), own_rows)
    near_context = near_attention(dealt, near, side)
    self_context = return_heads(near_context)
    hidden = jnp.concatenate(hidden, axis=1)
    folded = jnp.concatenate([hidden[: rows // 2], hidden[rows // 2 :]], axis=1)
    normed, side_normed, far_hidden = gather_rows(own_rows, folded, self_context)
    kv = keys_values(kv_weight, normed)
    self_context = after(self_context, side_normed[2])
    self_projected = jnp.dot(self_context, self_out_weight, preferred_element_type=F32)

    turn = jnp.stack([(y + k) % NY for k in range(NY)]).astype(jnp.int32)
    hidden_order = jnp.concatenate([turn * 2 + z, turn * 2 + 1 - z])
    cross_queries = project_queries([hidden, far_hidden], query_gain, cross_query_weight, hidden_order)
    later = next_ctx(cross_queries[:SPAN], -1)
    queries = jnp.concatenate([cross_queries[SPAN - 1 :], later[: SPAN - 1]], axis=0)

    counts = neighbour_counts.astype(jnp.int32)
    queries = after(queries, kv, self_projected)
    context, tail = attend_spans(queries, counts, kv, kv_weight, side_normed)
    earlier = next_ctx(tail, 1)
    half = rows // 2
    low = self_projected[half:] + jnp.dot(
        context[half - SPAN + 1 : rows - SPAN + 1], cross_out_weight, preferred_element_type=F32
    )
    low, low_far = split_z(low)
    cross_context = jnp.concatenate([earlier[1:], after(context, low_far)[: half - SPAN + 1]], axis=0)
    top = self_projected[:half] + jnp.dot(cross_context, cross_out_weight, preferred_element_type=F32)
    return (hidden_in.astype(F32) + scatter_sum(top, low, low_far)).astype(BF)


def solution(mesh):
    placed = (
        P("ctx", "enc"),
        P("ctx", "enc"),
        P("ctx", "enc"),
        P("ctx", "enc"),
        P(),
        P(),
        P(("enc", "ctx"), None),
        P(None, "enc"),
        P(None, None, "enc"),
        P("enc", None),
        P("enc", None),
        P("ctx", None, "enc"),
        P("ctx"),
    )
    return jax.shard_map(
        per_device, mesh=mesh, in_specs=placed, out_specs=P("ctx", "enc"), check_vma=False
    )
```
